32 devices in a mesh: gx: 4 (over x, core), gy: 2 (over y), ha: 4 (over z).
Axes of the slice: x: 2, y: 2, z: 4, core: 2. Of those that a mesh axis runs over, the one named last changes fastest.
Arguments:
- initial_value: float32 [64, 32, 4096], P('gx', 'gy', 'ha'), may hold values from -6 to 6
- corner: int32 [32, 4, 32], P(('gx', 'gy', 'ha')), may hold values from -1 to 244670, as said below
- weights: float32 [32, 16, 4, 32], P(('gx', 'gy', 'ha')), may hold values from 0 to 0.125
Outputs:
- final_value: float32 [64, 32, 4096], P('gx', 'gy', 'ha')
- sample_values: float32 [32, 4, 32], P(('gx', 'gy', 'ha'))
The draws below stay inside these ranges and needn't reach their ends.
Inputs may be any that keep to these rules, and one draw needn't show every extreme that they name: A live corner is ((a 16 + b) * 16 + k) * 64 + v with a <= 14, b <= 14, k <= 14, v <= 62; -1 marks an empty slot; in each bucket [s, :, o] the live slots come first; in every draw some owner's buckets are full from every source.
All inputs are finite; a program needn't handle non-finite values.
Results may differ from the reference program's by a relative error of at most 0.0003.
Values sent between devices are 32-bit elements; how exact they have to be, the bound alone decides.
A program may use at most 64 MiB of HBM per device.

```python
import jax
import jax.numpy as jnp
from jax import lax

CX = 16
CY = 16
CH = 16
NV = 64
STEPS = 4
CAP = 4
NX = 64
NY = 32
NH = 64
NHV = 4096
OWNERS = 32
N_GY = 2
N_HA = 4


def draw_corner(key, part):
    keys = jax.random.split(key, 7)
    bucket_fill = jax.random.randint(keys[0], (OWNERS, OWNERS), 0, CAP + 1)
    hot_owner = jax.random.randint(keys[1], (OWNERS,), 0, 4) == 0
    chosen_owner = jax.random.randint(keys[2], (), 0, OWNERS)
    hot_owner = hot_owner | (jnp.arange(OWNERS) == chosen_owner)
    bucket_fill = jnp.where(hot_owner[None, :], CAP, bucket_fill)
    empty_owner = (chosen_owner + 1) % OWNERS
    source_zero = jnp.arange(OWNERS)[:, None] == 0
    empty_mask = source_zero & (jnp.arange(OWNERS)[None, :] == empty_owner)
    bucket_fill = jnp.where(empty_mask, 0, bucket_fill)
    local_x = jax.random.randint(keys[3], (OWNERS, CAP, OWNERS), 0, CX - 1)
    local_y = jax.random.randint(keys[4], (OWNERS, CAP, OWNERS), 0, CY - 1)
    local_h = jax.random.randint(keys[5], (OWNERS, CAP, OWNERS), 0, CH - 1)
    local_v = jax.random.randint(keys[6], (OWNERS, CAP, OWNERS), 0, NV - 1)
    flat_cell = ((local_x * CY + local_y) * CH + local_h) * NV + local_v
    top_cell = (((CX - 2) * CY + CY - 2) * CH + CH - 2) * NV + NV - 2
    top_mask = (jnp.arange(OWNERS)[:, None, None] == 0) & (jnp.arange(CAP)[None, :, None] == 0) & (jnp.arange(OWNERS)[None, None, :] == chosen_owner)
    flat_cell = jnp.where(top_mask, top_cell, flat_cell)
    slot_index = jnp.arange(CAP)[None, :, None]
    live_slot = slot_index < bucket_fill[:, None, :]
    return jnp.where(live_slot, flat_cell, -1).astype(jnp.int32)


def block_scale(stream_key, extent, cuts, smallest, high):
    factor_of, own = 1.0, jax.random.fold_in(stream_key, 6)
    for dim, parts in cuts:
        draws = jnp.exp(jax.random.uniform(jax.random.fold_in(own, dim), (parts,), jnp.float32, smallest / len(cuts), high / len(cuts)))
        factor_of = factor_of * jnp.repeat(draws, extent[dim] // parts).reshape([-1 if axis == dim else 1 for axis in range(len(extent))])
    return factor_of


def noise(stream_key, extent, spread, reach, shards=(), kind=jnp.bfloat16):
    gain = block_scale(stream_key, extent, shards, -0.22, 0.18) if shards else 1.0
    drawn = jax.random.normal(stream_key, extent, jnp.float32) * spread * gain
    return jnp.minimum(jnp.maximum(drawn, -reach), reach).astype(kind)


def setup_inputs(seed: int = 0) -> dict:
    key_of = jax.random.split(jax.random.key(seed), 4)
    initial_value = noise(key_of[0], (NX, NY, NHV), 1.0, 6.0, ((0, 4), (1, 2), (2, 4)), jnp.float32)
    corner = draw_corner(jax.random.fold_in(key_of[3], 71), 0)
    weights = jnp.clip(0.125 * jax.random.uniform(key_of[2], (OWNERS, 16, CAP, OWNERS), jnp.float32) ** block_scale(key_of[2], (OWNERS, 16, CAP, OWNERS), ((0, 32),), -0.2, 0.2), 0.0, 0.125)
    return {"initial_value": initial_value, "corner": corner, "weights": weights}


epsilon = 1e-6
turn_rate = 1.0
time_step = 0.15
two_pi = 6.283185307179586


def window_of(array_in, begin_at, length_of, along, stride):
    return lax.slice_in_dim(array_in, begin_at * stride, (begin_at + length_of) * stride, axis=along)


def blend(outer_low, inner_low, center, inner_high, outer_high):
    guess_one = outer_low / 3.0 - 7.0 * inner_low / 6.0 + 11.0 * center / 6.0
    guess_two = -inner_low / 6.0 + 5.0 * center / 6.0 + inner_high / 3.0
    guess_three = center / 3.0 + 5.0 * inner_high / 6.0 - outer_high / 6.0
    rough_one = 13.0 / 12.0 * (outer_low - 2.0 * inner_low + center) ** 2 + 0.25 * (outer_low - 4.0 * inner_low + 3.0 * center) ** 2
    rough_two = 13.0 / 12.0 * (inner_low - 2.0 * center + inner_high) ** 2 + 0.25 * (inner_low - inner_high) ** 2
    rough_three = 13.0 / 12.0 * (center - 2.0 * inner_high + outer_high) ** 2 + 0.25 * (3.0 * center - 4.0 * inner_high + outer_high) ** 2
    weight_one = 0.1 / (rough_one + epsilon) ** 2
    weight_two = 0.6 / (rough_two + epsilon) ** 2
    weight_three = 0.3 / (rough_three + epsilon) ** 2
    return (weight_one * guess_one + weight_two * guess_two + weight_three * guess_three) / (weight_one + weight_two + weight_three)


def weno_pair(padded, along, stride, length_of):
    differences = window_of(padded, 1, length_of + 5, along, stride) - window_of(padded, 0, length_of + 5, along, stride)
    stencil = [window_of(differences, shift_at, length_of, along, stride) for shift_at in range(6)]
    slope_minus = blend(stencil[0], stencil[1], stencil[2], stencil[3], stencil[4])
    slope_plus = blend(stencil[5], stencil[4], stencil[3], stencil[2], stencil[1])
    return slope_minus, slope_plus


def drift_tables(first_heading, count_h, total_h):
    heading_index = first_heading + jnp.arange(count_h, dtype=jnp.int32)
    heading_angle = heading_index.astype(jnp.float32) * (two_pi / total_h)
    speeds = 0.5 + jnp.arange(NV, dtype=jnp.int32).astype(jnp.float32) / (NV - 1)
    drift_x = (jnp.cos(heading_angle)[:, None] * speeds[None, :]).reshape(-1)
    drift_y = (jnp.sin(heading_angle)[:, None] * speeds[None, :]).reshape(-1)
    return drift_x, drift_y


def advance(level_set, padded_x, padded_y, padded_h, drift_x, drift_y):
    count_x = level_set.shape[0]
    count_y = level_set.shape[1]
    count_h = level_set.shape[2] // NV
    xm_slope, xp_slope = weno_pair(padded_x, 0, 1, count_x)
    ym_slope, yp_slope = weno_pair(padded_y, 1, 1, count_y)
    hm_slope, hp_slope = weno_pair(padded_h, 2, NV, count_h)
    hamiltonian = drift_x * (0.5 * (xm_slope + xp_slope)) + drift_y * (0.5 * (ym_slope + yp_slope))
    hamiltonian = hamiltonian - turn_rate * jnp.abs(0.5 * (hm_slope + hp_slope))
    hamiltonian = hamiltonian - 0.5 * (jnp.abs(drift_x) * (xp_slope - xm_slope) + jnp.abs(drift_y) * (yp_slope - ym_slope) + turn_rate * (hp_slope - hm_slope))
    return level_set - time_step * jnp.maximum(hamiltonian, 0.0)


def reference(initial_value, corner, weights):
    drift_x, drift_y = drift_tables(0, NH, NH)
    level_set = initial_value
    for step_index in range(STEPS):
        padded_x = jnp.pad(level_set, ((3, 3), (0, 0), (0, 0)))
        padded_y = jnp.pad(level_set, ((0, 0), (3, 3), (0, 0)))
        padded_h = jnp.concatenate([level_set[:, :, NHV - 3 * NV:], level_set, level_set[:, :, :3 * NV]], axis=2)
        level_set = advance(level_set, padded_x, padded_y, padded_h, drift_x, drift_y)
    owners = jnp.arange(OWNERS, dtype=jnp.int32)
    owner_x = owners // (N_GY * N_HA)
    owner_y = (owners // N_HA) % N_GY
    owner_h = owners % N_HA
    live_slot = corner >= 0
    clamped = jnp.maximum(corner, 0)
    local_x = clamped // (CY * CH * NV)
    local_y = (clamped // (CH * NV)) % CY
    local_h = (clamped // NV) % CH
    local_v = clamped % NV
    base_index = ((owner_x[None, None, :] * CX + local_x) * NY + owner_y[None, None, :] * CY + local_y) * NHV
    base_index = base_index + (owner_h[None, None, :] * CH + local_h) * NV + local_v
    offset_list = []
    for bit_x in range(2):
        for bit_y in range(2):
            for bit_h in range(2):
                for bit_v in range(2):
                    offset_list.append(bit_x * NY * NHV + bit_y * NHV + bit_h * NV + bit_v)
    corner_offsets = jnp.array(offset_list, dtype=jnp.int32)
    flat_grid = level_set.reshape(-1)
    gathered = flat_grid[base_index[None] + corner_offsets[:, None, None, None]]
    weight_table = jnp.moveaxis(weights, 1, 0)
    sampled = jnp.sum(weight_table * gathered, axis=0)
    sample_values = jnp.where(live_slot, sampled, 0.0)
    return level_set, sample_values
```

```python
import functools

import jax
import jax.numpy as jnp
import numpy as np
from jax import lax
from jax.experimental import pallas as pl
from jax.experimental.pallas import tpu as pltpu
from jax.sharding import PartitionSpec as P

NV = 64
STEPS = 4
CAP = 4
MESH = pl.DeviceIdType.MESH
EPS4 = 4e-6
DT = 0.15
LO, HI = 3, 2


def smooth(t):
    return (13.0 / 3.0) * (t * t) + EPS4


def square(v):
    return v * v


def upwind_line(cells):
    n = len(cells)
    d = [cells[i + 1] - cells[i] for i in range(n - 1)]
    e = [d[i + 1] - d[i] for i in range(n - 2)]
    t = [e[i + 1] - e[i] for i in range(n - 3)]
    z = [t[i] - t[i + 1] for i in range(n - 4)]
    m = [smooth(v) for v in t]
    e3 = [3.0 * v for v in e]
    out = []
    for i in range(n - 5):
        s1 = square(m[i] + square(e3[i + 1] - e[i]))
        s2 = square(m[i + 1] + square(e[i + 1] + e[i + 2]))
        s3 = square(m[i + 2] + square(e3[i + 2] - e[i + 3]))
        bc = s2 * s3
        ab = 3.0 * (s1 * s2)
        w = bc + ab + 6.0 * (s1 * s3)
        num = (z[i] + z[i]) * bc + z[i + 1] * ab
        lin = 6.0 * d[i + 2] + (e[i + 1] + (e[i + 2] + e[i + 2]))
        out.append(lin + num * pl.reciprocal(w, approx=True))
    return out


def heading_term(u):
    d = [u[i + 1] - u[i] for i in range(6)]
    e = [d[i + 1] - d[i] for i in range(5)]
    t = [e[i + 1] - e[i] for i in range(4)]
    z = [t[i] - t[i + 1] for i in range(3)]
    m = [smooth(v) for v in t]
    e3 = [3.0 * v for v in e]

    def parts(i):
        s1 = square(m[i] + square(e3[i + 1] - e[i]))
        s2 = square(m[i + 1] + square(e[i + 1] + e[i + 2]))
        s3 = square(m[i + 2] + square(e3[i + 2] - e[i + 3]))
        return s1 * s2, s2 * s3, 6.0 * (s1 * s3)

    ab, bc, ac = parts(0)
    ab = 3.0 * ab
    num = (z[0] + z[0]) * bc + z[1] * ab
    minus = 6.0 * d[2] + (e[1] + (e[2] + e[2])) + num * pl.reciprocal(bc + ab + ac, approx=True)
    ab, bc, ac = parts(1)
    bc = 3.0 * bc
    num = (z[2] + z[2]) * ab + z[1] * bc
    negated = (e[3] + (e[2] + e[2])) - 6.0 * d[3] + num * pl.reciprocal(bc + ab + ac, approx=True)
    return jnp.minimum(minus, negated)


def kernel(sizes, v_hbm, code_ref, wt_ref, drift_ref, out_hbm, res_ref,
           grid, hxy, stage, send_h, recv_h, code_in, wt_in, code_s, wt_s, rows,
           in_sem, out_sem, halo_send, halo_recv, cs_sem, cr_sem, ws_sem, wr_sem, rs_sem, rr_sem, loc_sem):
    ngx, ngy, nha, cx, cy, nj = sizes
    total = ngx * ngy * nha
    gx, gy, ha = lax.axis_index("gx"), lax.axis_index("gy"), lax.axis_index("ha")
    me = (gx * ngy + gy) * nha + ha
    quarter = ha * 4 // nha
    east = (quarter == 0) | (quarter == 3)
    north = quarter < 2
    sx = jnp.where(east, 1, -1)
    sy = jnp.where(north, 1, -1)
    x0 = jnp.where(east, 0, cx - 1)
    y0 = jnp.where(north, 0, cy - 1)
    xb = jnp.where(east, 0, cx + 2 * LO - 1)
    yb = jnp.where(north, 0, cy + 2 * LO - 1)

    def near(forward, a, b, count):
        return pl.ds(jnp.where(forward, a, b), count)

    def up_dst(forward, c):
        return near(forward, 0, c + LO, LO)

    def up_src(forward, c):
        return near(forward, c, LO, LO)

    def down_dst(forward, c):
        return near(forward, c + LO, LO - HI, HI)

    def down_src(forward, c):
        return near(forward, LO, c + LO - HI, HI)


    def device_of(o):
        return (o // (ngy * nha), (o // nha) % ngy, o % nha)

    loads = [
        pltpu.make_async_copy(
            v_hbm.at[:, pl.ds(128 * j, 128)], stage.at[pl.ds(j * cx * cy, cx * cy)], in_sem.at[j])
        for j in range(nj)
    ]
    for c in loads:
        c.start()

    barrier = pltpu.get_barrier_semaphore()

    @pl.loop(1, total)
    def _(i):
        pl.semaphore_signal(barrier, inc=1, device_id=device_of((me + i) % total), device_id_type=MESH)

    tile0 = jnp.zeros((8, 128), jnp.float32)
    x_up = gx - sx
    x_down = gx + sx
    y_up = gy - sy
    y_down = gy + sy
    has_xu = (x_up >= 0) & (x_up < ngx)
    has_xd = (x_down >= 0) & (x_down < ngx)
    has_yu = (y_up >= 0) & (y_up < ngy)
    has_yd = (y_down >= 0) & (y_down < ngy)

    def zero_x(first, count):
        @pl.loop(0, STEPS)
        def _(n):
            @pl.loop(0, cy)
            def _(y):
                for x in range(count):
                    grid[n, y + LO, first + x, 8:16, :] = tile0

    def zero_y(first, count):
        @pl.loop(0, STEPS)
        def _(n):
            @pl.loop(0, cx)
            def _(x):
                for y in range(count):
                    grid[n, first + y, x + LO, 8:16, :] = tile0

    pl.when(jnp.logical_not(has_xu))(lambda: zero_x(jnp.where(east, 0, cx + LO), LO))
    pl.when(jnp.logical_not(has_xd))(lambda: zero_x(jnp.where(east, cx + LO, LO - HI), HI))
    pl.when(jnp.logical_not(has_yu))(lambda: zero_y(jnp.where(north, 0, cy + LO), LO))
    pl.when(jnp.logical_not(has_yd))(lambda: zero_y(jnp.where(north, cy + LO, LO - HI), HI))

    for c in loads:
        c.wait()

    @pl.loop(0, cy)
    def _(y):
        for x in range(cx):
            row = x * cy + y
            grid[0, y + LO, x + LO, 8:16, :] = stage[pl.ds(row, nj, stride=cx * cy), :]

    pl.semaphore_wait(barrier, total - 1)

    def request(o):
        return (
            pltpu.make_async_remote_copy(
                src_ref=code_ref.at[o], dst_ref=code_in.at[me], send_sem=cs_sem.at[o],
                recv_sem=cr_sem.at[me], device_id=device_of(o), device_id_type=MESH),
            pltpu.make_async_remote_copy(
                src_ref=wt_ref.at[o], dst_ref=wt_in.at[me], send_sem=ws_sem.at[o],
                recv_sem=wr_sem.at[me], device_id=device_of(o), device_id_type=MESH),
        )

    def request_from(o):
        return (
            pltpu.make_async_remote_copy(
                src_ref=code_ref.at[o], dst_ref=code_in.at[o], send_sem=cs_sem.at[o],
                recv_sem=cr_sem.at[o], device_id=device_of(o), device_id_type=MESH),
            pltpu.make_async_remote_copy(
                src_ref=wt_ref.at[o], dst_ref=wt_in.at[o], send_sem=ws_sem.at[o],
                recv_sem=wr_sem.at[o], device_id=device_of(o), device_id_type=MESH),
        )

    ys, xs = pl.ds(LO, cy), pl.ds(LO, cx)

    def x_copies(n):
        g = grid.at[n]
        up = pltpu.make_async_remote_copy(
            src_ref=g.at[ys, up_src(east, cx), pl.ds(8, 8)], dst_ref=g.at[ys, up_dst(east, cx), pl.ds(8, 8)],
            send_sem=halo_send.at[n, 0], recv_sem=halo_recv.at[n, 0],
            device_id=(x_down, gy, ha), device_id_type=MESH)
        down = pltpu.make_async_remote_copy(
            src_ref=g.at[ys, down_src(east, cx), pl.ds(8, 8)], dst_ref=g.at[ys, down_dst(east, cx), pl.ds(8, 8)],
            send_sem=halo_send.at[n, 1], recv_sem=halo_recv.at[n, 1],
            device_id=(x_up, gy, ha), device_id_type=MESH)
        return up, down

    def y_copies(n):
        g = grid.at[n]
        up = pltpu.make_async_remote_copy(
            src_ref=g.at[up_src(north, cy), xs, pl.ds(8, 8)], dst_ref=g.at[up_dst(north, cy), xs, pl.ds(8, 8)],
            send_sem=halo_send.at[n, 2], recv_sem=halo_recv.at[n, 2],
            device_id=(gx, y_down, ha), device_id_type=MESH)
        down = pltpu.make_async_remote_copy(
            src_ref=g.at[down_src(north, cy), xs, pl.ds(8, 8)], dst_ref=g.at[down_dst(north, cy), xs, pl.ds(8, 8)],
            send_sem=halo_send.at[n, 3], recv_sem=halo_recv.at[n, 3],
            device_id=(gx, y_up, ha), device_id_type=MESH)
        return up, down

    def h_copies(n):
        return tuple(
            pltpu.make_async_remote_copy(
                src_ref=send_h.at[n, k], dst_ref=recv_h.at[n, k],
                send_sem=halo_send.at[n, 4 + k], recv_sem=halo_recv.at[n, 4 + k],
                device_id=(gx, gy, (ha + (1 if k == 0 else nha - 1)) % nha), device_id_type=MESH)
            for k in range(2))

    low_half = lax.broadcasted_iota(jnp.int32, (8, 128), 1) < NV

    def swap(v):
        return pltpu.roll(v, NV, 1)

    flat = grid.reshape(grid.shape[0] * grid.shape[1] * grid.shape[2] * 24, 128)

    def row_of(n, y, x, r):
        return ((n * (cy + 2 * LO) + y + LO) * (cx + 2 * LO) + x + LO) * 24 + r

    halves = cx // 16

    def send(n):
        @pl.loop(0, cy)
        def _(y):
            for q in range(2 * halves):
                send_h[n, 0, y * 2 * halves + q] = flat[pl.ds(row_of(n, y, 8 * q, 15), 8, stride=24), :]
                send_h[n, 1, y * 2 * halves + q] = flat[pl.ds(row_of(n, y, 8 * q, 8), 8, stride=24), :]
            for q in range(halves):
                a = flat[pl.ds(row_of(n, y, 16 * q, 14), 8, stride=24), :]
                b = flat[pl.ds(row_of(n, y, 16 * q + 8, 14), 8, stride=24), :]
                send_h[n, 0, cy * 2 * halves + y * halves + q] = jnp.where(low_half, swap(a), b)
                a = flat[pl.ds(row_of(n, y, 16 * q, 9), 8, stride=24), :]
                b = flat[pl.ds(row_of(n, y, 16 * q + 8, 9), 8, stride=24), :]
                send_h[n, 1, cy * 2 * halves + y * halves + q] = jnp.where(low_half, a, swap(b))

        for c in h_copies(n):
            c.start()
        xu, xd = x_copies(n)
        yu, yd = y_copies(n)
        pl.when(has_yd)(lambda: yu.start())
        pl.when(has_yu)(lambda: yd.start())
        pl.when(has_xd)(lambda: xu.start())
        pl.when(has_xu)(lambda: xd.start())

    def unpack(n):
        @pl.loop(0, cy)
        def _(y):
            for q in range(2 * halves):
                flat[pl.ds(row_of(n, y, 8 * q, 7), 8, stride=24), :] = recv_h[n, 0, y * 2 * halves + q]
                flat[pl.ds(row_of(n, y, 8 * q, 16), 8, stride=24), :] = recv_h[n, 1, y * 2 * halves + q]
            for q in range(halves):
                v = recv_h[n, 0, cy * 2 * halves + y * halves + q]
                flat[pl.ds(row_of(n, y, 16 * q, 6), 8, stride=24), :] = swap(v)
                flat[pl.ds(row_of(n, y, 16 * q + 8, 6), 8, stride=24), :] = v
                v = recv_h[n, 1, cy * 2 * halves + y * halves + q]
                flat[pl.ds(row_of(n, y, 16 * q, 17), 8, stride=24), :] = v
                flat[pl.ds(row_of(n, y, 16 * q + 8, 17), 8, stride=24), :] = swap(v)

    send(0)

    @pl.loop(1, total)
    def _(i):
        for c in request((me + i) % total):
            c.start()

    own = (pltpu.make_async_copy(code_ref.at[me], code_in.at[me], loc_sem.at[0]),
           pltpu.make_async_copy(wt_ref.at[me], wt_in.at[me], loc_sem.at[1]))
    for c in own:
        c.start()
    for c in own:
        c.wait()

    drift_x = drift_ref[ha, 0]
    drift_y = drift_ref[ha, 1]

    @pl.loop(0, STEPS)
    def _(n):
        yu, yd = y_copies(n)
        pl.when(has_yu)(lambda: yu.wait_recv())
        pl.when(has_yd)(lambda: yd.wait_recv())

        @pl.loop(0, cx)
        def _(x):
            line = upwind_line([grid[n, yb + sy * i, x + LO, 8:16, :] for i in range(LO + cy + HI)])
            for y in range(cy):
                hxy[y0 + sy * y, x] = drift_y * line[y]

        xu, xd = x_copies(n)
        pl.when(has_xu)(lambda: xu.wait_recv())
        pl.when(has_xd)(lambda: xd.wait_recv())

        @pl.loop(0, cy)
        def _(y):
            line = upwind_line([grid[n, y + LO, xb + sx * i, 8:16, :] for i in range(LO + cx + HI)])
            for x in range(cx):
                hxy[y, x0 + sx * x] += drift_x * line[x]

        for c in h_copies(n):
            c.wait_recv()
        unpack(n)

        @pl.loop(0, cy)
        def _(y):
            for x in range(cx):
                g = [grid[n, y + LO, x + LO, pl.ds(r, 8), :] for r in range(6, 11)]
                s = [swap(v) for v in g]
                odd = [jnp.where(low_half, s[i], s[i + 1]) for i in range(4)]
                term = heading_term([odd[0], g[1], odd[1], g[2], odd[2], g[3], odd[3]])
                ham = hxy[y, x] + (DT / 6.0) * term
                grid[n + 1, y + LO, x + LO, 8:16, :] = g[2] - jnp.maximum(ham, 0.0)

        pl.when(n < STEPS - 1)(lambda: send(n + 1))

    @pl.loop(0, cy)
    def _(y):
        for x in range(cx):
            row = x * cy + y
            stage[pl.ds(row, nj, stride=cx * cy), :] = grid[STEPS, y + LO, x + LO, 8:16, :]

    stores = [
        pltpu.make_async_copy(
            stage.at[pl.ds(j * cx * cy, cx * cy)], out_hbm.at[:, pl.ds(128 * j, 128)], out_sem.at[j])
        for j in range(nj)
    ]
    for c in stores:
        c.start()

    @pl.loop(1, total)
    def _(i):
        for c in request_from((me + i) % total):
            c.wait()

    to_s = (pltpu.make_async_copy(code_in, code_s, loc_sem.at[0]),
            pltpu.make_async_copy(wt_in, wt_s, loc_sem.at[1]))
    for c in to_s:
        c.start()
    for c in to_s:
        c.wait()

    ramp = (lax.broadcasted_iota(jnp.int32, (8, 128), 0) * 128
            + lax.broadcasted_iota(jnp.int32, (8, 128), 1))
    hv = nj * 128

    def answer(o, slot_of):
        return pltpu.make_async_remote_copy(
            src_ref=rows.at[o], dst_ref=res_ref.at[slot_of], send_sem=rs_sem.at[o],
            recv_sem=rr_sem.at[slot_of], device_id=device_of(o), device_id_type=MESH)

    @pl.loop(0, total)
    def _(i):
        o = (me + i + 1) % total
        for slot in range(CAP):
            c = jnp.maximum(code_s[o, 0, slot], 0)
            a = c // (cy * hv)
            b = (c // hv) % cy
            at = ramp - c % hv
            hits = [at == off for off in (0, 1, NV, NV + 1)]
            acc = None
            for i1 in range(2):
                for i2 in range(2):
                    w = jnp.zeros((8, 128), jnp.float32)
                    for k in range(4):
                        w = jnp.where(hits[k], wt_s[o, 0, slot * 16 + 8 * i1 + 4 * i2 + k], w)
                    part = w * grid[STEPS, b + i2 + LO, a + i1 + LO, 8:16, :]
                    acc = part if acc is None else acc + part
            rows[o, slot:slot + 1, :] = jnp.sum(acc, axis=0, keepdims=True)
        pl.when(o != me)(lambda: answer(o, me).start())

    mine = pltpu.make_async_copy(rows.at[me], res_ref.at[me], loc_sem.at[2])
    mine.start()
    mine.wait()

    @pl.loop(1, total)
    def _(i):
        o = (me + i) % total
        answer(o, o).wait()

    @pl.loop(0, STEPS)
    def _(n):
        xu, xd = x_copies(n)
        yu, yd = y_copies(n)
        pl.when(has_yd)(lambda: yu.wait_send())
        pl.when(has_yu)(lambda: yd.wait_send())
        pl.when(has_xd)(lambda: xu.wait_send())
        pl.when(has_xu)(lambda: xd.wait_send())
        for c in h_copies(n):
            c.wait_send()

    for c in stores:
        c.wait()


def drift_table(nha, ch, nj):
    heads = nha * ch
    angle = np.arange(heads, dtype=np.int32).astype(np.float32) * np.float32(6.283185307179586 / heads)
    speed = np.float32(0.5) + np.arange(NV, dtype=np.float32) / np.float32(NV - 1)
    quarter = np.arange(heads) * 4 // heads
    sign_x = np.where((quarter == 0) | (quarter == 3), 1.0, -1.0).astype(np.float32)
    sign_y = np.where(quarter < 2, 1.0, -1.0).astype(np.float32)
    table = np.stack([(sign_x * np.cos(angle))[:, None] * speed, (sign_y * np.sin(angle))[:, None] * speed])
    table = table * np.float32(DT / 6.0)
    return table.reshape(2, nha, nj, 128).transpose(1, 0, 2, 3).astype(np.float32)


def solution(mesh):
    ngx, ngy, nha = (mesh.shape[k] for k in ("gx", "gy", "ha"))
    total = ngx * ngy * nha
    assert nha % 4 == 0

    def local(initial_value, corner, weights):
        cx, cy, chv = initial_value.shape
        nj = chv // 128
        assert nj == 8 and cx % 16 == 0
        table = jnp.asarray(drift_table(nha, chv // NV, nj))
        codes = jnp.pad(corner[0].T, ((0, 0), (0, 128 - CAP))).reshape(total, 1, 128)
        wts = weights[0].transpose(2, 1, 0).reshape(total, CAP * 16)
        wts = jnp.pad(wts, ((0, 0), (0, 128 - CAP * 16))).reshape(total, 1, 128)
        f32, i32 = jnp.float32, jnp.int32
        tiles = cy * (cx // 16) * 3
        dma = pltpu.SemaphoreType.DMA
        vmem = pl.BlockSpec(memory_space=pltpu.VMEM)
        any_ = pl.BlockSpec(memory_space=pl.ANY)
        final, parts = pl.pallas_call(
            functools.partial(kernel, (ngx, ngy, nha, cx, cy, nj)),
            out_shape=(jax.ShapeDtypeStruct((cx * cy, chv), f32),
                       jax.ShapeDtypeStruct((total, CAP, 128), f32)),
            in_specs=[any_, vmem, vmem, vmem],
            out_specs=(any_, vmem),
            scratch_shapes=[
                pltpu.VMEM((STEPS + 1, cy + 2 * LO, cx + 2 * LO, 24, 128), f32),
                pltpu.VMEM((cy, cx, 8, 128), f32),
                pltpu.VMEM((nj * cx * cy, 128), f32),
                pltpu.VMEM((STEPS, 2, tiles, 8, 128), f32),
                pltpu.VMEM((STEPS, 2, tiles, 8, 128), f32),
                pltpu.VMEM((total, 1, 128), i32),
                pltpu.VMEM((total, 1, 128), f32),
                pltpu.SMEM((total, 1, 128), i32),
                pltpu.SMEM((total, 1, 128), f32),
                pltpu.VMEM((total, CAP, 128), f32),
                dma((nj,)), dma((nj,)), dma((STEPS, 6)), dma((STEPS, 6)),
                dma((total,)), dma((total,)), dma((total,)), dma((total,)),
                dma((total,)), dma((total,)), dma((3,)),
            ],
            compiler_params=pltpu.CompilerParams(
                collective_id=0, has_side_effects=True, vmem_limit_bytes=56 * 1024 * 1024),
        )(initial_value.reshape(cx * cy, chv), codes, wts, table)
        sampled = jnp.sum(parts, axis=2).T[None]
        return (final.reshape(cx, cy, chv), jnp.where(corner >= 0, sampled, 0.0))

    return jax.shard_map(
        local,
        mesh=mesh,
        in_specs=(P("gx", "gy", "ha"), P(("gx", "gy", "ha"), None, None),
                  P(("gx", "gy", "ha"), None, None, None)),
        out_specs=(P("gx", "gy", "ha"), P(("gx", "gy", "ha"), None, None)),
        check_vma=False,
    )
```

```python
import functools

import jax
import jax.numpy as jnp
import numpy as np
from jax import lax
from jax.experimental import pallas as pl
from jax.experimental.pallas import tpu as pltpu
from jax.sharding import PartitionSpec as P

NV = 64
STEPS = 4
CAP = 4
MESH = pl.DeviceIdType.MESH
EPS4 = 4e-6
DT = 0.15
LO, HI = 3, 2
CHUNKS = 4


def smooth(t):
    return (13.0 / 3.0) * (t * t) + EPS4


def square(v):
    return v * v


def upwind_line(cells):
    n = len(cells)
    d = [cells[i + 1] - cells[i] for i in range(n - 1)]
    e = [d[i + 1] - d[i] for i in range(n - 2)]
    t = [e[i + 1] - e[i] for i in range(n - 3)]
    z = [t[i] - t[i + 1] for i in range(n - 4)]
    m = [smooth(v) for v in t]
    e3 = [3.0 * v for v in e]
    out = []
    for i in range(n - 5):
        s1 = square(m[i] + square(e3[i + 1] - e[i]))
        s2 = square(m[i + 1] + square(e[i + 1] + e[i + 2]))
        s3 = square(m[i + 2] + square(e3[i + 2] - e[i + 3]))
        bc = s2 * s3
        ab = 3.0 * (s1 * s2)
        w = bc + ab + 6.0 * (s1 * s3)
        num = (z[i] + z[i]) * bc + z[i + 1] * ab
        lin = 6.0 * d[i + 2] + (e[i + 1] + (e[i + 2] + e[i + 2]))
        out.append(lin + num * pl.reciprocal(w, approx=True))
    return out


def heading_term(u):
    d = [u[i + 1] - u[i] for i in range(6)]
    e = [d[i + 1] - d[i] for i in range(5)]
    t = [e[i + 1] - e[i] for i in range(4)]
    z = [t[i] - t[i + 1] for i in range(3)]
    m = [smooth(v) for v in t]
    e3 = [3.0 * v for v in e]

    def parts(i):
        s1 = square(m[i] + square(e3[i + 1] - e[i]))
        s2 = square(m[i + 1] + square(e[i + 1] + e[i + 2]))
        s3 = square(m[i + 2] + square(e3[i + 2] - e[i + 3]))
        return s1 * s2, s2 * s3, 6.0 * (s1 * s3)

    ab, bc, ac = parts(0)
    ab = 3.0 * ab
    num = (z[0] + z[0]) * bc + z[1] * ab
    minus = 6.0 * d[2] + (e[1] + (e[2] + e[2])) + num * pl.reciprocal(bc + ab + ac, approx=True)
    ab, bc, ac = parts(1)
    bc = 3.0 * bc
    num = (z[2] + z[2]) * ab + z[1] * bc
    negated = (e[3] + (e[2] + e[2])) - 6.0 * d[3] + num * pl.reciprocal(bc + ab + ac, approx=True)
    return jnp.minimum(minus, negated)


def kernel(sizes, v_hbm, code_ref, wt_ref, drift_ref, out_hbm, res_ref,
           grid, hx, hy, stage, send_h, recv_h, code_in, wt_in, code_s, wt_s, rows,
           in_sem, out_sem, halo_send, halo_recv, cs_sem, cr_sem, ws_sem, wr_sem, rs_sem, rr_sem, loc_sem):
    ngx, ngy, nha, cx, cy, nj = sizes
    total = ngx * ngy * nha
    gx, gy, ha = lax.axis_index("gx"), lax.axis_index("gy"), lax.axis_index("ha")
    me = (gx * ngy + gy) * nha + ha
    quarter = ha * 4 // nha
    east = (quarter == 0) | (quarter == 3)
    north = quarter < 2
    sx = jnp.where(east, 1, -1)
    sy = jnp.where(north, 1, -1)
    x0 = jnp.where(east, 0, cx - 1)
    y0 = jnp.where(north, 0, cy - 1)
    xb = jnp.where(east, 0, cx + 2 * LO - 1)
    yb = jnp.where(north, 0, cy + 2 * LO - 1)

    def near(forward, a, b, count):
        return pl.ds(jnp.where(forward, a, b), count)

    def up_dst(forward, c):
        return near(forward, 0, c + LO, LO)

    def up_src(forward, c):
        return near(forward, c, LO, LO)

    def down_dst(forward, c):
        return near(forward, c + LO, LO - HI, HI)

    def down_src(forward, c):
        return near(forward, LO, c + LO - HI, HI)


    def device_of(o):
        return (o // (ngy * nha), (o // nha) % ngy, o % nha)

    loads = [
        pltpu.make_async_copy(
            v_hbm.at[:, pl.ds(128 * j, 128)], stage.at[pl.ds(j * cx * cy, cx * cy)], in_sem.at[j])
        for j in range(nj)
    ]
    for c in loads:
        c.start()

    barrier = pltpu.get_barrier_semaphore()

    @pl.loop(1, total)
    def _(i):
        pl.semaphore_signal(barrier, inc=1, device_id=device_of((me + i) % total), device_id_type=MESH)

    tile0 = jnp.zeros((8, 128), jnp.float32)
    x_up = gx - sx
    x_down = gx + sx
    y_up = gy - sy
    y_down = gy + sy
    has_xu = (x_up >= 0) & (x_up < ngx)
    has_xd = (x_down >= 0) & (x_down < ngx)
    has_yu = (y_up >= 0) & (y_up < ngy)
    has_yd = (y_down >= 0) & (y_down < ngy)

    def zero_x(first, count):
        @pl.loop(0, STEPS)
        def _(n):
            @pl.loop(0, cy)
            def _(y):
                for x in range(count):
                    grid[n, y + LO, first + x, 8:16, :] = tile0

    def zero_y(first, count):
        @pl.loop(0, STEPS)
        def _(n):
            @pl.loop(0, cx)
            def _(x):
                for y in range(count):
                    grid[n, first + y, x + LO, 8:16, :] = tile0

    pl.when(jnp.logical_not(has_xu))(lambda: zero_x(jnp.where(east, 0, cx + LO), LO))
    pl.when(jnp.logical_not(has_xd))(lambda: zero_x(jnp.where(east, cx + LO, LO - HI), HI))
    pl.when(jnp.logical_not(has_yu))(lambda: zero_y(jnp.where(north, 0, cy + LO), LO))
    pl.when(jnp.logical_not(has_yd))(lambda: zero_y(jnp.where(north, cy + LO, LO - HI), HI))

    for c in loads:
        c.wait()

    @pl.loop(0, cy)
    def _(y):
        for x in range(cx):
            row = x * cy + y
            grid[0, y + LO, x + LO, 8:16, :] = stage[pl.ds(row, nj, stride=cx * cy), :]

    pl.semaphore_wait(barrier, total - 1)

    def request(o):
        return (
            pltpu.make_async_remote_copy(
                src_ref=code_ref.at[o], dst_ref=code_in.at[me], send_sem=cs_sem.at[o],
                recv_sem=cr_sem.at[me], device_id=device_of(o), device_id_type=MESH),
            pltpu.make_async_remote_copy(
                src_ref=wt_ref.at[o], dst_ref=wt_in.at[me], send_sem=ws_sem.at[o],
                recv_sem=wr_sem.at[me], device_id=device_of(o), device_id_type=MESH),
        )

    def request_from(o):
        return (
            pltpu.make_async_remote_copy(
                src_ref=code_ref.at[o], dst_ref=code_in.at[o], send_sem=cs_sem.at[o],
                recv_sem=cr_sem.at[o], device_id=device_of(o), device_id_type=MESH),
            pltpu.make_async_remote_copy(
                src_ref=wt_ref.at[o], dst_ref=wt_in.at[o], send_sem=ws_sem.at[o],
                recv_sem=wr_sem.at[o], device_id=device_of(o), device_id_type=MESH),
        )

    ys, xs = pl.ds(LO, cy), pl.ds(LO, cx)

    def x_copies(n):
        g = grid.at[n]
        up = pltpu.make_async_remote_copy(
            src_ref=g.at[ys, up_src(east, cx), pl.ds(8, 8)], dst_ref=g.at[ys, up_dst(east, cx), pl.ds(8, 8)],
            send_sem=halo_send.at[n, 0], recv_sem=halo_recv.at[n, 0],
            device_id=(x_down, gy, ha), device_id_type=MESH)
        down = pltpu.make_async_remote_copy(
            src_ref=g.at[ys, down_src(east, cx), pl.ds(8, 8)], dst_ref=g.at[ys, down_dst(east, cx), pl.ds(8, 8)],
            send_sem=halo_send.at[n, 1], recv_sem=halo_recv.at[n, 1],
            device_id=(x_up, gy, ha), device_id_type=MESH)
        return up, down

    def y_copies(n):
        g = grid.at[n]
        up = pltpu.make_async_remote_copy(
            src_ref=g.at[up_src(north, cy), xs, pl.ds(8, 8)], dst_ref=g.at[up_dst(north, cy), xs, pl.ds(8, 8)],
            send_sem=halo_send.at[n, 2], recv_sem=halo_recv.at[n, 2],
            device_id=(gx, y_down, ha), device_id_type=MESH)
        down = pltpu.make_async_remote_copy(
            src_ref=g.at[down_src(north, cy), xs, pl.ds(8, 8)], dst_ref=g.at[down_dst(north, cy), xs, pl.ds(8, 8)],
            send_sem=halo_send.at[n, 3], recv_sem=halo_recv.at[n, 3],
            device_id=(gx, y_up, ha), device_id_type=MESH)
        return up, down

    def h_copies(n, c):
        return tuple(
            pltpu.make_async_remote_copy(
                src_ref=send_h.at[n, k, c], dst_ref=recv_h.at[n, k, c],
                send_sem=halo_send.at[n, 4 + k * CHUNKS + c], recv_sem=halo_recv.at[n, 4 + k * CHUNKS + c],
                device_id=(gx, gy, (ha + (1 if k == 0 else nha - 1)) % nha), device_id_type=MESH)
            for k in range(2))

    low_half = lax.broadcasted_iota(jnp.int32, (8, 128), 1) < NV

    def swap(v):
        return pltpu.roll(v, NV, 1)

    flat = grid.reshape(grid.shape[0] * grid.shape[1] * grid.shape[2] * 24, 128)

    def row_of(n, y, x, r):
        return ((n * (cy + 2 * LO) + y + LO) * (cx + 2 * LO) + x + LO) * 24 + r

    halves = cx // 16
    depth = cy // CHUNKS

    def pack(n, c, r):
        y = c * depth + r
        for q in range(2 * halves):
            send_h[n, 0, c, r * 2 * halves + q] = flat[pl.ds(row_of(n, y, 8 * q, 15), 8, stride=24), :]
            send_h[n, 1, c, r * 2 * halves + q] = flat[pl.ds(row_of(n, y, 8 * q, 8), 8, stride=24), :]
        for q in range(halves):
            at = (2 * depth + r) * halves + q
            a = flat[pl.ds(row_of(n, y, 16 * q, 14), 8, stride=24), :]
            b = flat[pl.ds(row_of(n, y, 16 * q + 8, 14), 8, stride=24), :]
            send_h[n, 0, c, at] = jnp.where(low_half, swap(a), b)
            a = flat[pl.ds(row_of(n, y, 16 * q, 9), 8, stride=24), :]
            b = flat[pl.ds(row_of(n, y, 16 * q + 8, 9), 8, stride=24), :]
            send_h[n, 1, c, at] = jnp.where(low_half, a, swap(b))

    def unpack(n, c, r):
        y = c * depth + r
        for q in range(2 * halves):
            flat[pl.ds(row_of(n, y, 8 * q, 7), 8, stride=24), :] = recv_h[n, 0, c, r * 2 * halves + q]
            flat[pl.ds(row_of(n, y, 8 * q, 16), 8, stride=24), :] = recv_h[n, 1, c, r * 2 * halves + q]
        for q in range(halves):
            at = (2 * depth + r) * halves + q
            v = recv_h[n, 0, c, at]
            flat[pl.ds(row_of(n, y, 16 * q, 6), 8, stride=24), :] = swap(v)
            flat[pl.ds(row_of(n, y, 16 * q + 8, 6), 8, stride=24), :] = v
            v = recv_h[n, 1, c, at]
            flat[pl.ds(row_of(n, y, 16 * q, 17), 8, stride=24), :] = v
            flat[pl.ds(row_of(n, y, 16 * q + 8, 17), 8, stride=24), :] = swap(v)

    def send_chunk(n, c):
        for copy in h_copies(n, c):
            copy.start()

    def send_y(n):
        yu, yd = y_copies(n)
        pl.when(has_yd)(lambda: yu.start())
        pl.when(has_yu)(lambda: yd.start())

    def send_x(n):
        xu, xd = x_copies(n)
        pl.when(has_xd)(lambda: xu.start())
        pl.when(has_xu)(lambda: xd.start())

    def chunk_at(i):
        return (i + CHUNKS - 1) % CHUNKS

    send_y(0)
    send_x(0)

    @pl.loop(0, CHUNKS)
    def _(i):
        c = chunk_at(i)

        @pl.loop(0, depth)
        def _(r):
            pack(0, c, r)

        send_chunk(0, c)

    @pl.loop(1, total)
    def _(i):
        for c in request((me + i) % total):
            c.start()

    own = (pltpu.make_async_copy(code_ref.at[me], code_in.at[me], loc_sem.at[0]),
           pltpu.make_async_copy(wt_ref.at[me], wt_in.at[me], loc_sem.at[1]))
    for c in own:
        c.start()
    for c in own:
        c.wait()

    drift_x = drift_ref[ha, 0]
    drift_y = drift_ref[ha, 1]

    def y_part(n, first, count):
        @pl.loop(0, cx)
        def _(x):
            line = upwind_line([grid[n, yb + sy * i, x + LO, 8:16, :] for i in range(first, first + count + 5)])
            for k in range(count):
                hy[y0 + sy * (first + k), x] = drift_y * line[k]

    def x_part(n, first, count):
        @pl.loop(0, cy)
        def _(y):
            line = upwind_line([grid[n, y + LO, xb + sx * i, 8:16, :] for i in range(first, first + count + 5)])
            for k in range(count):
                hx[y, x0 + sx * (first + k)] = drift_x * line[k]

    @pl.loop(0, STEPS)
    def _(n):
        y_part(n, LO, cy - LO - HI)
        x_part(n, LO, cx - LO - HI)

        yu, yd = y_copies(n)
        pl.when(has_yu)(lambda: yu.wait_recv())
        pl.when(has_yd)(lambda: yd.wait_recv())
        y_part(n, 0, LO)
        y_part(n, cy - HI, HI)

        xu, xd = x_copies(n)
        pl.when(has_xu)(lambda: xu.wait_recv())
        pl.when(has_xd)(lambda: xd.wait_recv())
        x_part(n, 0, LO)
        x_part(n, cx - HI, HI)

        @pl.loop(0, CHUNKS)
        def _(i):
            c = chunk_at(i)
            for copy in h_copies(n, c):
                copy.wait_recv()

            @pl.loop(0, depth)
            def _(r):
                y = c * depth + r
                unpack(n, c, r)
                for x in range(cx):
                    g = [grid[n, y + LO, x + LO, pl.ds(r, 8), :] for r in range(6, 11)]
                    s = [swap(v) for v in g]
                    odd = [jnp.where(low_half, s[i], s[i + 1]) for i in range(4)]
                    term = heading_term([odd[0], g[1], odd[1], g[2], odd[2], g[3], odd[3]])
                    ham = hx[y, x] + hy[y, x] + (DT / 6.0) * term
                    grid[n + 1, y + LO, x + LO, 8:16, :] = g[2] - jnp.maximum(ham, 0.0)
                pl.when(n < STEPS - 1)(lambda: pack(n + 1, c, r))

            pl.when(n < STEPS - 1)(lambda: send_chunk(n + 1, c))
            pl.when((n < STEPS - 1) & (i == 1))(lambda: send_y(n + 1))

        pl.when(n < STEPS - 1)(lambda: send_x(n + 1))

    @pl.loop(0, cy)
    def _(y):
        for x in range(cx):
            row = x * cy + y
            stage[pl.ds(row, nj, stride=cx * cy), :] = grid[STEPS, y + LO, x + LO, 8:16, :]

    stores = [
        pltpu.make_async_copy(
            stage.at[pl.ds(j * cx * cy, cx * cy)], out_hbm.at[:, pl.ds(128 * j, 128)], out_sem.at[j])
        for j in range(nj)
    ]
    for c in stores:
        c.start()

    @pl.loop(1, total)
    def _(i):
        for c in request_from((me + i) % total):
            c.wait()

    to_s = (pltpu.make_async_copy(code_in, code_s, loc_sem.at[0]),
            pltpu.make_async_copy(wt_in, wt_s, loc_sem.at[1]))
    for c in to_s:
        c.start()
    for c in to_s:
        c.wait()

    ramp = (lax.broadcasted_iota(jnp.int32, (8, 128), 0) * 128
            + lax.broadcasted_iota(jnp.int32, (8, 128), 1))
    hv = nj * 128

    def answer(o, slot_of):
        return pltpu.make_async_remote_copy(
            src_ref=rows.at[o], dst_ref=res_ref.at[slot_of], send_sem=rs_sem.at[o],
            recv_sem=rr_sem.at[slot_of], device_id=device_of(o), device_id_type=MESH)

    @pl.loop(0, total)
    def _(i):
        o = (me + i + 1) % total
        for slot in range(CAP):
            c = jnp.maximum(code_s[o, 0, slot], 0)
            a = c // (cy * hv)
            b = (c // hv) % cy
            at = ramp - c % hv
            hits = [at == off for off in (0, 1, NV, NV + 1)]
            acc = None
            for i1 in range(2):
                for i2 in range(2):
                    w = jnp.zeros((8, 128), jnp.float32)
                    for k in range(4):
                        w = jnp.where(hits[k], wt_s[o, 0, slot * 16 + 8 * i1 + 4 * i2 + k], w)
                    part = w * grid[STEPS, b + i2 + LO, a + i1 + LO, 8:16, :]
                    acc = part if acc is None else acc + part
            rows[o, slot:slot + 1, :] = jnp.sum(acc, axis=0, keepdims=True)
        pl.when(o != me)(lambda: answer(o, me).start())

    mine = pltpu.make_async_copy(rows.at[me], res_ref.at[me], loc_sem.at[2])
    mine.start()
    mine.wait()

    @pl.loop(1, total)
    def _(i):
        o = (me + i) % total
        answer(o, o).wait()

    @pl.loop(0, STEPS)
    def _(n):
        xu, xd = x_copies(n)
        yu, yd = y_copies(n)
        pl.when(has_yd)(lambda: yu.wait_send())
        pl.when(has_yu)(lambda: yd.wait_send())
        pl.when(has_xd)(lambda: xu.wait_send())
        pl.when(has_xu)(lambda: xd.wait_send())
        for c in range(CHUNKS):
            for copy in h_copies(n, c):
                copy.wait_send()

    for c in stores:
        c.wait()


def drift_table(nha, ch, nj):
    heads = nha * ch
    angle = np.arange(heads, dtype=np.int32).astype(np.float32) * np.float32(6.283185307179586 / heads)
    speed = np.float32(0.5) + np.arange(NV, dtype=np.float32) / np.float32(NV - 1)
    quarter = np.arange(heads) * 4 // heads
    sign_x = np.where((quarter == 0) | (quarter == 3), 1.0, -1.0).astype(np.float32)
    sign_y = np.where(quarter < 2, 1.0, -1.0).astype(np.float32)
    table = np.stack([(sign_x * np.cos(angle))[:, None] * speed, (sign_y * np.sin(angle))[:, None] * speed])
    table = table * np.float32(DT / 6.0)
    return table.reshape(2, nha, nj, 128).transpose(1, 0, 2, 3).astype(np.float32)


def solution(mesh):
    ngx, ngy, nha = (mesh.shape[k] for k in ("gx", "gy", "ha"))
    total = ngx * ngy * nha
    assert nha % 4 == 0

    def local(initial_value, corner, weights):
        cx, cy, chv = initial_value.shape
        nj = chv // 128
        assert nj == 8 and cx % 16 == 0
        table = jnp.asarray(drift_table(nha, chv // NV, nj))
        codes = jnp.pad(corner[0].T, ((0, 0), (0, 128 - CAP))).reshape(total, 1, 128)
        wts = weights[0].transpose(2, 1, 0).reshape(total, CAP * 16)
        wts = jnp.pad(wts, ((0, 0), (0, 128 - CAP * 16))).reshape(total, 1, 128)
        f32, i32 = jnp.float32, jnp.int32
        tiles = cy * (cx // 16) * 3
        dma = pltpu.SemaphoreType.DMA
        vmem = pl.BlockSpec(memory_space=pltpu.VMEM)
        any_ = pl.BlockSpec(memory_space=pl.ANY)
        final, parts = pl.pallas_call(
            functools.partial(kernel, (ngx, ngy, nha, cx, cy, nj)),
            out_shape=(jax.ShapeDtypeStruct((cx * cy, chv), f32),
                       jax.ShapeDtypeStruct((total, CAP, 128), f32)),
            in_specs=[any_, vmem, vmem, vmem],
            out_specs=(any_, vmem),
            scratch_shapes=[
                pltpu.VMEM((STEPS + 1, cy + 2 * LO, cx + 2 * LO, 24, 128), f32),
                pltpu.VMEM((cy, cx, 8, 128), f32),
                pltpu.VMEM((cy, cx, 8, 128), f32),
                pltpu.VMEM((nj * cx * cy, 128), f32),
                pltpu.VMEM((STEPS, 2, CHUNKS, tiles // CHUNKS, 8, 128), f32),
                pltpu.VMEM((STEPS, 2, CHUNKS, tiles // CHUNKS, 8, 128), f32),
                pltpu.VMEM((total, 1, 128), i32),
                pltpu.VMEM((total, 1, 128), f32),
                pltpu.SMEM((total, 1, 128), i32),
                pltpu.SMEM((total, 1, 128), f32),
                pltpu.VMEM((total, CAP, 128), f32),
                dma((nj,)), dma((nj,)), dma((STEPS, 4 + 2 * CHUNKS)), dma((STEPS, 4 + 2 * CHUNKS)),
                dma((total,)), dma((total,)), dma((total,)), dma((total,)),
                dma((total,)), dma((total,)), dma((3,)),
            ],
            compiler_params=pltpu.CompilerParams(
                collective_id=0, has_side_effects=True, vmem_limit_bytes=56 * 1024 * 1024),
        )(initial_value.reshape(cx * cy, chv), codes, wts, table)
        sampled = jnp.sum(parts, axis=2).T[None]
        return (final.reshape(cx, cy, chv), jnp.where(corner >= 0, sampled, 0.0))

    return jax.shard_map(
        local,
        mesh=mesh,
        in_specs=(P("gx", "gy", "ha"), P(("gx", "gy", "ha"), None, None),
                  P(("gx", "gy", "ha"), None, None, None)),
        out_specs=(P("gx", "gy", "ha"), P(("gx", "gy", "ha"), None, None)),
        check_vma=False,
    )
```

```python
import functools

import jax
import jax.numpy as jnp
import numpy as np
from jax import lax
from jax.experimental import pallas as pl
from jax.experimental.pallas import tpu as pltpu
from jax.sharding import PartitionSpec as P

NV = 64
STEPS = 4
CAP = 4
MESH = pl.DeviceIdType.MESH
EPS4 = 4e-6
DT = 0.15
LO, HI = 3, 2
CHUNKS = 4


def smooth(t):
    return (13.0 / 3.0) * (t * t) + EPS4


def weight(v):
    v = pl.reciprocal(v, approx=True)
    return v * v


def terms(cells):
    n = len(cells)
    d = [cells[i + 1] - cells[i] for i in range(n - 1)]
    e = [d[i + 1] - d[i] for i in range(n - 2)]
    t = [e[i + 1] - e[i] for i in range(n - 3)]
    z = [t[i] - t[i + 1] for i in range(n - 4)]
    m = [smooth(v) for v in t]
    e3 = [3.0 * v for v in e]
    return d, e, z, m, e3


def weights_at(i, e, m, e3):
    u1 = e3[i + 1] - e[i]
    u2 = e[i + 1] + e[i + 2]
    u3 = e3[i + 2] - e[i + 3]
    return weight(m[i] + u1 * u1), 6.0 * weight(m[i + 1] + u2 * u2), weight(m[i + 2] + u3 * u3)


def upwind_line(cells):
    d, e, z, m, e3 = terms(cells)
    out = []
    for i in range(len(cells) - 5):
        g1, g2, g3 = weights_at(i, e, m, e3)
        g3 = 3.0 * g3
        num = (z[i] + z[i]) * g1 + z[i + 1] * g3
        lin = 6.0 * d[i + 2] + (e[i + 1] + (e[i + 2] + e[i + 2]))
        out.append(lin + num * pl.reciprocal(g1 + g2 + g3, approx=True))
    return out


def both_ways(cells):
    d, e, z, m, e3 = terms(cells)
    g1, g2, g3 = weights_at(0, e, m, e3)
    c = 6.0 * d[2]
    h1, h3 = 3.0 * g1, 3.0 * g3
    forward = (c + (e[1] + (e[2] + e[2]))
               + ((z[0] + z[0]) * g1 + z[1] * h3) * pl.reciprocal(g1 + g2 + h3, approx=True))
    negated = ((e[2] + (e[1] + e[1])) - c
               + ((z[1] + z[1]) * g3 + z[0] * h1) * pl.reciprocal(h1 + g2 + g3, approx=True))
    return forward, negated


def kernel(sizes, v_hbm, code_ref, wt_ref, drift_ref, out_hbm, res_ref,
           grid, hx, hy, moved, stage, send_h, recv_h, code_in, wt_in, code_s, wt_s, rows,
           in_sem, out_sem, halo_send, halo_recv, cs_sem, cr_sem, ws_sem, wr_sem, rs_sem, rr_sem, loc_sem):
    ngx, ngy, nha, cx, cy, nj = sizes
    total = ngx * ngy * nha
    gx, gy, ha = lax.axis_index("gx"), lax.axis_index("gy"), lax.axis_index("ha")
    me = (gx * ngy + gy) * nha + ha
    quarter = ha * 4 // nha
    east = (quarter == 0) | (quarter == 3)
    north = quarter < 2
    sx = jnp.where(east, 1, -1)
    sy = jnp.where(north, 1, -1)
    x0 = jnp.where(east, 0, cx - 1)
    y0 = jnp.where(north, 0, cy - 1)
    xb = jnp.where(east, 0, cx + 2 * LO - 1)
    yb = jnp.where(north, 0, cy + 2 * LO - 1)

    def near(forward, a, b, count):
        return pl.ds(jnp.where(forward, a, b), count)

    def up_dst(forward, c):
        return near(forward, 0, c + LO, LO)

    def up_src(forward, c):
        return near(forward, c, LO, LO)

    def down_dst(forward, c):
        return near(forward, c + LO, LO - HI, HI)

    def down_src(forward, c):
        return near(forward, LO, c + LO - HI, HI)


    def device_of(o):
        return (o // (ngy * nha), (o // nha) % ngy, o % nha)

    loads = [
        pltpu.make_async_copy(
            v_hbm.at[:, pl.ds(128 * j, 128)], stage.at[pl.ds(j * cx * cy, cx * cy)], in_sem.at[j])
        for j in range(nj)
    ]
    for c in loads:
        c.start()

    barrier = pltpu.get_barrier_semaphore()

    @pl.loop(1, total)
    def _(i):
        pl.semaphore_signal(barrier, inc=1, device_id=device_of((me + i) % total), device_id_type=MESH)

    tile0 = jnp.zeros((8, 128), jnp.float32)
    x_up = gx - sx
    x_down = gx + sx
    y_up = gy - sy
    y_down = gy + sy
    has_xu = (x_up >= 0) & (x_up < ngx)
    has_xd = (x_down >= 0) & (x_down < ngx)
    has_yu = (y_up >= 0) & (y_up < ngy)
    has_yd = (y_down >= 0) & (y_down < ngy)

    def zero_x(first, count):
        @pl.loop(0, STEPS)
        def _(n):
            @pl.loop(0, cy)
            def _(y):
                for x in range(count):
                    grid[n, y + LO, first + x, 8:16, :] = tile0

    def zero_y(first, count):
        @pl.loop(0, STEPS)
        def _(n):
            @pl.loop(0, cx)
            def _(x):
                for y in range(count):
                    grid[n, first + y, x + LO, 8:16, :] = tile0

    pl.when(jnp.logical_not(has_xu))(lambda: zero_x(jnp.where(east, 0, cx + LO), LO))
    pl.when(jnp.logical_not(has_xd))(lambda: zero_x(jnp.where(east, cx + LO, LO - HI), HI))
    pl.when(jnp.logical_not(has_yu))(lambda: zero_y(jnp.where(north, 0, cy + LO), LO))
    pl.when(jnp.logical_not(has_yd))(lambda: zero_y(jnp.where(north, cy + LO, LO - HI), HI))

    for c in loads:
        c.wait()

    @pl.loop(0, cy)
    def _(y):
        for x in range(cx):
            row = x * cy + y
            grid[0, y + LO, x + LO, 8:16, :] = stage[pl.ds(row, nj, stride=cx * cy), :]

    pl.semaphore_wait(barrier, total - 1)

    def request(o):
        return (
            pltpu.make_async_remote_copy(
                src_ref=code_ref.at[o], dst_ref=code_in.at[me], send_sem=cs_sem.at[o],
                recv_sem=cr_sem.at[me], device_id=device_of(o), device_id_type=MESH),
            pltpu.make_async_remote_copy(
                src_ref=wt_ref.at[o], dst_ref=wt_in.at[me], send_sem=ws_sem.at[o],
                recv_sem=wr_sem.at[me], device_id=device_of(o), device_id_type=MESH),
        )

    def request_from(o):
        return (
            pltpu.make_async_remote_copy(
                src_ref=code_ref.at[o], dst_ref=code_in.at[o], send_sem=cs_sem.at[o],
                recv_sem=cr_sem.at[o], device_id=device_of(o), device_id_type=MESH),
            pltpu.make_async_remote_copy(
                src_ref=wt_ref.at[o], dst_ref=wt_in.at[o], send_sem=ws_sem.at[o],
                recv_sem=wr_sem.at[o], device_id=device_of(o), device_id_type=MESH),
        )

    ys, xs = pl.ds(LO, cy), pl.ds(LO, cx)

    def x_copies(n):
        g = grid.at[n]
        up = pltpu.make_async_remote_copy(
            src_ref=g.at[ys, up_src(east, cx), pl.ds(8, 8)], dst_ref=g.at[ys, up_dst(east, cx), pl.ds(8, 8)],
            send_sem=halo_send.at[n, 0], recv_sem=halo_recv.at[n, 0],
            device_id=(x_down, gy, ha), device_id_type=MESH)
        down = pltpu.make_async_remote_copy(
            src_ref=g.at[ys, down_src(east, cx), pl.ds(8, 8)], dst_ref=g.at[ys, down_dst(east, cx), pl.ds(8, 8)],
            send_sem=halo_send.at[n, 1], recv_sem=halo_recv.at[n, 1],
            device_id=(x_up, gy, ha), device_id_type=MESH)
        return up, down

    def y_copies(n):
        g = grid.at[n]
        up = pltpu.make_async_remote_copy(
            src_ref=g.at[up_src(north, cy), xs, pl.ds(8, 8)], dst_ref=g.at[up_dst(north, cy), xs, pl.ds(8, 8)],
            send_sem=halo_send.at[n, 2], recv_sem=halo_recv.at[n, 2],
            device_id=(gx, y_down, ha), device_id_type=MESH)
        down = pltpu.make_async_remote_copy(
            src_ref=g.at[down_src(north, cy), xs, pl.ds(8, 8)], dst_ref=g.at[down_dst(north, cy), xs, pl.ds(8, 8)],
            send_sem=halo_send.at[n, 3], recv_sem=halo_recv.at[n, 3],
            device_id=(gx, y_up, ha), device_id_type=MESH)
        return up, down

    def h_copies(n, c):
        return tuple(
            pltpu.make_async_remote_copy(
                src_ref=send_h.at[n, k, c], dst_ref=recv_h.at[n, k, c],
                send_sem=halo_send.at[n, 4 + k * CHUNKS + c], recv_sem=halo_recv.at[n, 4 + k * CHUNKS + c],
                device_id=(gx, gy, (ha + (1 if k == 0 else nha - 1)) % nha), device_id_type=MESH)
            for k in range(2))

    low_half = lax.broadcasted_iota(jnp.int32, (8, 128), 1) < NV

    def swap(v):
        return pltpu.roll(v, NV, 1)

    flat = grid.reshape(grid.shape[0] * grid.shape[1] * grid.shape[2] * 24, 128)

    moved_flat = moved.reshape(cx * 24, 128)

    def row_of(n, y, x, r):
        return ((n * (cy + 2 * LO) + y + LO) * (cx + 2 * LO) + x + LO) * 24 + r

    halves = cx // 16
    depth = cy // CHUNKS

    def pack(n, c, r):
        y = c * depth + r
        for q in range(2 * halves):
            send_h[n, 0, c, r * 2 * halves + q] = flat[pl.ds(row_of(n, y, 8 * q, 15), 8, stride=24), :]
            send_h[n, 1, c, r * 2 * halves + q] = flat[pl.ds(row_of(n, y, 8 * q, 8), 8, stride=24), :]
        for q in range(halves):
            at = (2 * depth + r) * halves + q
            a = flat[pl.ds(row_of(n, y, 16 * q, 14), 8, stride=24), :]
            b = flat[pl.ds(row_of(n, y, 16 * q + 8, 14), 8, stride=24), :]
            send_h[n, 0, c, at] = jnp.where(low_half, swap(a), b)
            a = flat[pl.ds(row_of(n, y, 16 * q, 9), 8, stride=24), :]
            b = flat[pl.ds(row_of(n, y, 16 * q + 8, 9), 8, stride=24), :]
            send_h[n, 1, c, at] = jnp.where(low_half, a, swap(b))

    def unpack(n, c, r):
        y = c * depth + r
        for q in range(2 * halves):
            flat[pl.ds(row_of(n, y, 8 * q, 7), 8, stride=24), :] = recv_h[n, 0, c, r * 2 * halves + q]
            flat[pl.ds(row_of(n, y, 8 * q, 16), 8, stride=24), :] = recv_h[n, 1, c, r * 2 * halves + q]
        for q in range(halves):
            at = (2 * depth + r) * halves + q
            v = recv_h[n, 0, c, at]
            here = [send_h[n, 1, c, r * 2 * halves + 2 * q + k] for k in range(2)]
            past = [recv_h[n, 0, c, r * 2 * halves + 2 * q + k] for k in range(2)]
            edge, _ = both_ways([
                v,
                jnp.where(low_half, past[0], swap(past[1])), jnp.where(low_half, swap(past[0]), past[1]),
                jnp.where(low_half, here[0], swap(here[1])), jnp.where(low_half, swap(here[0]), here[1]),
                send_h[n, 1, c, at],
            ])
            moved_flat[pl.ds(16 * q * 24 + 7, 8, stride=24), :] = edge
            moved_flat[pl.ds((16 * q + 8) * 24 + 7, 8, stride=24), :] = swap(edge)
            v = recv_h[n, 1, c, at]
            flat[pl.ds(row_of(n, y, 16 * q, 17), 8, stride=24), :] = v
            flat[pl.ds(row_of(n, y, 16 * q + 8, 17), 8, stride=24), :] = swap(v)

    def send_chunk(n, c):
        for copy in h_copies(n, c):
            copy.start()

    def send_y(n):
        yu, yd = y_copies(n)
        pl.when(has_yd)(lambda: yu.start())
        pl.when(has_yu)(lambda: yd.start())

    def send_x(n):
        xu, xd = x_copies(n)
        pl.when(has_xd)(lambda: xu.start())
        pl.when(has_xu)(lambda: xd.start())

    def chunk_at(i):
        return (i + CHUNKS - 1) % CHUNKS

    send_y(0)
    send_x(0)

    @pl.loop(0, CHUNKS)
    def _(i):
        c = chunk_at(i)

        @pl.loop(0, depth)
        def _(r):
            pack(0, c, r)

        send_chunk(0, c)

    @pl.loop(1, total)
    def _(i):
        for c in request((me + i) % total):
            c.start()

    own = (pltpu.make_async_copy(code_ref.at[me], code_in.at[me], loc_sem.at[0]),
           pltpu.make_async_copy(wt_ref.at[me], wt_in.at[me], loc_sem.at[1]))
    for c in own:
        c.start()
    for c in own:
        c.wait()

    drift_x = drift_ref[ha, 0]
    drift_y = drift_ref[ha, 1]

    def y_part(n, first, count):
        @pl.loop(0, cx)
        def _(x):
            line = upwind_line([grid[n, yb + sy * i, x + LO, 8:16, :] for i in range(first, first + count + 5)])
            for k in range(count):
                hy[y0 + sy * (first + k), x] = drift_y * line[k]

    def x_part(n, first, count):
        @pl.loop(0, cy)
        def _(y):
            line = upwind_line([grid[n, y + LO, xb + sx * i, 8:16, :] for i in range(first, first + count + 5)])
            for k in range(count):
                hx[y, x0 + sx * (first + k)] = drift_x * line[k]

    @pl.loop(0, STEPS)
    def _(n):
        y_part(n, LO, cy - LO - HI)
        x_part(n, LO, cx - LO - HI)

        yu, yd = y_copies(n)
        pl.when(has_yu)(lambda: yu.wait_recv())
        pl.when(has_yd)(lambda: yd.wait_recv())
        y_part(n, 0, LO)
        y_part(n, cy - HI, HI)

        xu, xd = x_copies(n)
        pl.when(has_xu)(lambda: xu.wait_recv())
        pl.when(has_xd)(lambda: xd.wait_recv())
        x_part(n, 0, LO)
        x_part(n, cx - HI, HI)

        @pl.loop(0, CHUNKS)
        def _(i):
            c = chunk_at(i)
            for copy in h_copies(n, c):
                copy.wait_recv()

            @pl.loop(0, depth)
            def _(r):
                y = c * depth + r
                unpack(n, c, r)
                for x in range(cx):
                    g = [grid[n, y + LO, x + LO, pl.ds(k, 8), :] for k in range(7, 11)]
                    s = [swap(v) for v in g]
                    odd = [jnp.where(low_half, s[k], s[k + 1]) for k in range(3)]
                    forward, negated = both_ways([g[0], odd[0], g[1], odd[1], g[2], odd[2]])
                    forward = swap(forward)
                    moved[x, 8:16, :] = forward
                    forward = jnp.where(low_half, moved[x, 7:15, :], forward)
                    term = jnp.minimum(forward, negated)
                    ham = hx[y, x] + hy[y, x] + (DT / 6.0) * term
                    grid[n + 1, y + LO, x + LO, 8:16, :] = g[1] - jnp.maximum(ham, 0.0)
                pl.when(n < STEPS - 1)(lambda: pack(n + 1, c, r))

            pl.when(n < STEPS - 1)(lambda: send_chunk(n + 1, c))
            pl.when((n < STEPS - 1) & (i == 1))(lambda: send_y(n + 1))

        pl.when(n < STEPS - 1)(lambda: send_x(n + 1))

    @pl.loop(0, cy)
    def _(y):
        for x in range(cx):
            row = x * cy + y
            stage[pl.ds(row, nj, stride=cx * cy), :] = grid[STEPS, y + LO, x + LO, 8:16, :]

    stores = [
        pltpu.make_async_copy(
            stage.at[pl.ds(j * cx * cy, cx * cy)], out_hbm.at[:, pl.ds(128 * j, 128)], out_sem.at[j])
        for j in range(nj)
    ]
    for c in stores:
        c.start()

    @pl.loop(1, total)
    def _(i):
        for c in request_from((me + i) % total):
            c.wait()

    to_s = (pltpu.make_async_copy(code_in, code_s, loc_sem.at[0]),
            pltpu.make_async_copy(wt_in, wt_s, loc_sem.at[1]))
    for c in to_s:
        c.start()
    for c in to_s:
        c.wait()

    ramp = (lax.broadcasted_iota(jnp.int32, (8, 128), 0) * 128
            + lax.broadcasted_iota(jnp.int32, (8, 128), 1))
    hv = nj * 128

    def answer(o, slot_of):
        return pltpu.make_async_remote_copy(
            src_ref=rows.at[o], dst_ref=res_ref.at[slot_of], send_sem=rs_sem.at[o],
            recv_sem=rr_sem.at[slot_of], device_id=device_of(o), device_id_type=MESH)

    @pl.loop(0, total)
    def _(i):
        o = (me + i + 1) % total
        for slot in range(CAP):
            c = jnp.maximum(code_s[o, 0, slot], 0)
            a = c // (cy * hv)
            b = (c // hv) % cy
            at = ramp - c % hv
            hits = [at == off for off in (0, 1, NV, NV + 1)]
            acc = None
            for i1 in range(2):
                for i2 in range(2):
                    w = jnp.zeros((8, 128), jnp.float32)
                    for k in range(4):
                        w = jnp.where(hits[k], wt_s[o, 0, slot * 16 + 8 * i1 + 4 * i2 + k], w)
                    part = w * grid[STEPS, b + i2 + LO, a + i1 + LO, 8:16, :]
                    acc = part if acc is None else acc + part
            rows[o, slot:slot + 1, :] = jnp.sum(acc, axis=0, keepdims=True)
        pl.when(o != me)(lambda: answer(o, me).start())

    mine = pltpu.make_async_copy(rows.at[me], res_ref.at[me], loc_sem.at[2])
    mine.start()
    mine.wait()

    @pl.loop(1, total)
    def _(i):
        o = (me + i) % total
        answer(o, o).wait()

    @pl.loop(0, STEPS)
    def _(n):
        xu, xd = x_copies(n)
        yu, yd = y_copies(n)
        pl.when(has_yd)(lambda: yu.wait_send())
        pl.when(has_yu)(lambda: yd.wait_send())
        pl.when(has_xd)(lambda: xu.wait_send())
        pl.when(has_xu)(lambda: xd.wait_send())
        for c in range(CHUNKS):
            for copy in h_copies(n, c):
                copy.wait_send()

    for c in stores:
        c.wait()


def drift_table(nha, ch, nj):
    heads = nha * ch
    angle = np.arange(heads, dtype=np.int32).astype(np.float32) * np.float32(6.283185307179586 / heads)
    speed = np.float32(0.5) + np.arange(NV, dtype=np.float32) / np.float32(NV - 1)
    quarter = np.arange(heads) * 4 // heads
    sign_x = np.where((quarter == 0) | (quarter == 3), 1.0, -1.0).astype(np.float32)
    sign_y = np.where(quarter < 2, 1.0, -1.0).astype(np.float32)
    table = np.stack([(sign_x * np.cos(angle))[:, None] * speed, (sign_y * np.sin(angle))[:, None] * speed])
    table = table * np.float32(DT / 6.0)
    return table.reshape(2, nha, nj, 128).transpose(1, 0, 2, 3).astype(np.float32)


def solution(mesh):
    ngx, ngy, nha = (mesh.shape[k] for k in ("gx", "gy", "ha"))
    total = ngx * ngy * nha
    assert nha % 4 == 0

    def local(initial_value, corner, weights):
        cx, cy, chv = initial_value.shape
        nj = chv // 128
        assert nj == 8 and cx % 16 == 0
        table = jnp.asarray(drift_table(nha, chv // NV, nj))
        codes = jnp.pad(corner[0].T, ((0, 0), (0, 128 - CAP))).reshape(total, 1, 128)
        wts = weights[0].transpose(2, 1, 0).reshape(total, CAP * 16)
        wts = jnp.pad(wts, ((0, 0), (0, 128 - CAP * 16))).reshape(total, 1, 128)
        f32, i32 = jnp.float32, jnp.int32
        tiles = cy * (cx // 16) * 3
        dma = pltpu.SemaphoreType.DMA
        vmem = pl.BlockSpec(memory_space=pltpu.VMEM)
        any_ = pl.BlockSpec(memory_space=pl.ANY)
        final, parts = pl.pallas_call(
            functools.partial(kernel, (ngx, ngy, nha, cx, cy, nj)),
            out_shape=(jax.ShapeDtypeStruct((cx * cy, chv), f32),
                       jax.ShapeDtypeStruct((total, CAP, 128), f32)),
            in_specs=[any_, vmem, vmem, vmem],
            out_specs=(any_, vmem),
            scratch_shapes=[
                pltpu.VMEM((STEPS + 1, cy + 2 * LO, cx + 2 * LO, 24, 128), f32),
                pltpu.VMEM((cy, cx, 8, 128), f32),
                pltpu.VMEM((cy, cx, 8, 128), f32),
                pltpu.VMEM((cx, 24, 128), f32),
                pltpu.VMEM((nj * cx * cy, 128), f32),
                pltpu.VMEM((STEPS, 2, CHUNKS, tiles // CHUNKS, 8, 128), f32),
                pltpu.VMEM((STEPS, 2, CHUNKS, tiles // CHUNKS, 8, 128), f32),
                pltpu.VMEM((total, 1, 128), i32),
                pltpu.VMEM((total, 1, 128), f32),
                pltpu.SMEM((total, 1, 128), i32),
                pltpu.SMEM((total, 1, 128), f32),
                pltpu.VMEM((total, CAP, 128), f32),
                dma((nj,)), dma((nj,)), dma((STEPS, 4 + 2 * CHUNKS)), dma((STEPS, 4 + 2 * CHUNKS)),
                dma((total,)), dma((total,)), dma((total,)), dma((total,)),
                dma((total,)), dma((total,)), dma((3,)),
            ],
            compiler_params=pltpu.CompilerParams(
                collective_id=0, has_side_effects=True, vmem_limit_bytes=56 * 1024 * 1024),
        )(initial_value.reshape(cx * cy, chv), codes, wts, table)
        sampled = jnp.sum(parts, axis=2).T[None]
        return (final.reshape(cx, cy, chv), jnp.where(corner >= 0, sampled, 0.0))

    return jax.shard_map(
        local,
        mesh=mesh,
        in_specs=(P("gx", "gy", "ha"), P(("gx", "gy", "ha"), None, None),
                  P(("gx", "gy", "ha"), None, None, None)),
        out_specs=(P("gx", "gy", "ha"), P(("gx", "gy", "ha"), None, None)),
        check_vma=False,
    )
```

```python
import functools

import jax
import jax.numpy as jnp
import numpy as np
from jax import lax
from jax.experimental import pallas as pl
from jax.experimental.pallas import tpu as pltpu
from jax.sharding import PartitionSpec as P

NV = 64
STEPS = 4
CAP = 4
MESH = pl.DeviceIdType.MESH
EPS4 = 4e-6
DT = 0.15
LO, HI = 3, 2
CHUNKS = 4


def smooth(t):
    return (13.0 / 3.0) * (t * t) + EPS4


def weight(v):
    v = pl.reciprocal(v, approx=True)
    return v * v


def terms(cells):
    n = len(cells)
    d = [cells[i + 1] - cells[i] for i in range(n - 1)]
    e = [d[i + 1] - d[i] for i in range(n - 2)]
    t = [e[i + 1] - e[i] for i in range(n - 3)]
    z = [t[i] - t[i + 1] for i in range(n - 4)]
    m = [smooth(v) for v in t]
    e3 = [3.0 * v for v in e]
    return d, e, z, m, e3


def weights_at(i, e, m, e3):
    u1 = e3[i + 1] - e[i]
    u2 = e[i + 1] + e[i + 2]
    u3 = e3[i + 2] - e[i + 3]
    return weight(m[i] + u1 * u1), 6.0 * weight(m[i + 1] + u2 * u2), weight(m[i + 2] + u3 * u3)


def upwind_line(cells):
    d, e, z, m, e3 = terms(cells)
    out = []
    for i in range(len(cells) - 5):
        g1, g2, g3 = weights_at(i, e, m, e3)
        g3 = 3.0 * g3
        num = (z[i] + z[i]) * g1 + z[i + 1] * g3
        lin = 6.0 * d[i + 2] + (e[i + 1] + (e[i + 2] + e[i + 2]))
        out.append(lin + num * pl.reciprocal(g1 + g2 + g3, approx=True))
    return out


def both_ways(cells):
    d, e, z, m, e3 = terms(cells)
    g1, g2, g3 = weights_at(0, e, m, e3)
    c = 6.0 * d[2]
    h1, h3 = 3.0 * g1, 3.0 * g3
    forward = (c + (e[1] + (e[2] + e[2]))
               + ((z[0] + z[0]) * g1 + z[1] * h3) * pl.reciprocal(g1 + g2 + h3, approx=True))
    negated = ((e[2] + (e[1] + e[1])) - c
               + ((z[1] + z[1]) * g3 + z[0] * h1) * pl.reciprocal(h1 + g2 + g3, approx=True))
    return forward, negated


def kernel(sizes, v_hbm, code_ref, wt_ref, drift_ref, out_hbm, res_ref,
           grid, hx, hy, moved, stage, send_h, recv_h, code_in, wt_in, code_s, wt_s, rows,
           in_sem, out_sem, halo_send, halo_recv, cs_sem, cr_sem, ws_sem, wr_sem, rs_sem, rr_sem, loc_sem):
    ngx, ngy, nha, cx, cy, nj = sizes
    total = ngx * ngy * nha
    gx, gy, ha = lax.axis_index("gx"), lax.axis_index("gy"), lax.axis_index("ha")
    me = (gx * ngy + gy) * nha + ha
    quarter = ha * 4 // nha
    east = (quarter == 0) | (quarter == 3)
    north = quarter < 2
    sx = jnp.where(east, 1, -1)
    sy = jnp.where(north, 1, -1)
    x0 = jnp.where(east, 0, cx - 1)
    y0 = jnp.where(north, 0, cy - 1)
    xb = jnp.where(east, 0, cx + 2 * LO - 1)
    yb = jnp.where(north, 0, cy + 2 * LO - 1)

    def near(forward, a, b, count):
        return pl.ds(jnp.where(forward, a, b), count)

    def up_dst(forward, c):
        return near(forward, 0, c + LO, LO)

    def up_src(forward, c):
        return near(forward, c, LO, LO)

    def down_dst(forward, c):
        return near(forward, c + LO, LO - HI, HI)

    def down_src(forward, c):
        return near(forward, LO, c + LO - HI, HI)


    def device_of(o):
        return (o // (ngy * nha), (o // nha) % ngy, o % nha)

    loads = [
        pltpu.make_async_copy(
            v_hbm.at[:, pl.ds(128 * j, 128)], stage.at[pl.ds(j * cx * cy, cx * cy)], in_sem.at[j])
        for j in range(nj)
    ]
    for c in loads:
        c.start()

    barrier = pltpu.get_barrier_semaphore()

    @pl.loop(1, total)
    def _(i):
        pl.semaphore_signal(barrier, inc=1, device_id=device_of((me + i) % total), device_id_type=MESH)

    tile0 = jnp.zeros((8, 128), jnp.float32)
    x_up = gx - sx
    x_down = gx + sx
    y_up = gy - sy
    y_down = gy + sy
    has_xu = (x_up >= 0) & (x_up < ngx)
    has_xd = (x_down >= 0) & (x_down < ngx)
    has_yu = (y_up >= 0) & (y_up < ngy)
    has_yd = (y_down >= 0) & (y_down < ngy)

    def zero_x(first, count):
        @pl.loop(0, STEPS)
        def _(n):
            @pl.loop(0, cy)
            def _(y):
                for x in range(count):
                    grid[n, y + LO, first + x, 8:16, :] = tile0

    def zero_y(first, count):
        @pl.loop(0, STEPS)
        def _(n):
            @pl.loop(0, cx)
            def _(x):
                for y in range(count):
                    grid[n, first + y, x + LO, 8:16, :] = tile0

    pl.when(jnp.logical_not(has_xu))(lambda: zero_x(jnp.where(east, 0, cx + LO), LO))
    pl.when(jnp.logical_not(has_xd))(lambda: zero_x(jnp.where(east, cx + LO, LO - HI), HI))
    pl.when(jnp.logical_not(has_yu))(lambda: zero_y(jnp.where(north, 0, cy + LO), LO))
    pl.when(jnp.logical_not(has_yd))(lambda: zero_y(jnp.where(north, cy + LO, LO - HI), HI))

    for c in loads:
        c.wait()

    @pl.loop(0, cy)
    def _(y):
        for x in range(cx):
            row = x * cy + y
            grid[0, y + LO, x + LO, 8:16, :] = stage[pl.ds(row, nj, stride=cx * cy), :]

    pl.semaphore_wait(barrier, total - 1)

    def request(o):
        return (
            pltpu.make_async_remote_copy(
                src_ref=code_ref.at[o], dst_ref=code_in.at[me], send_sem=cs_sem.at[o],
                recv_sem=cr_sem.at[me], device_id=device_of(o), device_id_type=MESH),
            pltpu.make_async_remote_copy(
                src_ref=wt_ref.at[o], dst_ref=wt_in.at[me], send_sem=ws_sem.at[o],
                recv_sem=wr_sem.at[me], device_id=device_of(o), device_id_type=MESH),
        )

    def request_from(o):
        return (
            pltpu.make_async_remote_copy(
                src_ref=code_ref.at[o], dst_ref=code_in.at[o], send_sem=cs_sem.at[o],
                recv_sem=cr_sem.at[o], device_id=device_of(o), device_id_type=MESH),
            pltpu.make_async_remote_copy(
                src_ref=wt_ref.at[o], dst_ref=wt_in.at[o], send_sem=ws_sem.at[o],
                recv_sem=wr_sem.at[o], device_id=device_of(o), device_id_type=MESH),
        )

    xs = pl.ds(LO, cx)
    depth = cy // CHUNKS

    def x_copies(n, c):
        g = grid.at[n]
        ys = pl.ds(LO + c * depth, depth)
        up = pltpu.make_async_remote_copy(
            src_ref=g.at[ys, up_src(east, cx), pl.ds(8, 8)], dst_ref=g.at[ys, up_dst(east, cx), pl.ds(8, 8)],
            send_sem=halo_send.at[n, 2 + c], recv_sem=halo_recv.at[n, 2 + c],
            device_id=(x_down, gy, ha), device_id_type=MESH)
        down = pltpu.make_async_remote_copy(
            src_ref=g.at[ys, down_src(east, cx), pl.ds(8, 8)], dst_ref=g.at[ys, down_dst(east, cx), pl.ds(8, 8)],
            send_sem=halo_send.at[n, 2 + CHUNKS + c], recv_sem=halo_recv.at[n, 2 + CHUNKS + c],
            device_id=(x_up, gy, ha), device_id_type=MESH)
        return up, down

    def y_copies(n):
        g = grid.at[n]
        up = pltpu.make_async_remote_copy(
            src_ref=g.at[up_src(north, cy), xs, pl.ds(8, 8)], dst_ref=g.at[up_dst(north, cy), xs, pl.ds(8, 8)],
            send_sem=halo_send.at[n, 0], recv_sem=halo_recv.at[n, 0],
            device_id=(gx, y_down, ha), device_id_type=MESH)
        down = pltpu.make_async_remote_copy(
            src_ref=g.at[down_src(north, cy), xs, pl.ds(8, 8)], dst_ref=g.at[down_dst(north, cy), xs, pl.ds(8, 8)],
            send_sem=halo_send.at[n, 1], recv_sem=halo_recv.at[n, 1],
            device_id=(gx, y_up, ha), device_id_type=MESH)
        return up, down

    def h_copies(n, c):
        return tuple(
            pltpu.make_async_remote_copy(
                src_ref=send_h.at[n, k, c], dst_ref=recv_h.at[n, k, c],
                send_sem=halo_send.at[n, 2 + (2 + k) * CHUNKS + c], recv_sem=halo_recv.at[n, 2 + (2 + k) * CHUNKS + c],
                device_id=(gx, gy, (ha + (1 if k == 0 else nha - 1)) % nha), device_id_type=MESH)
            for k in range(2))

    low_half = lax.broadcasted_iota(jnp.int32, (8, 128), 1) < NV

    def swap(v):
        return pltpu.roll(v, NV, 1)

    flat = grid.reshape(grid.shape[0] * grid.shape[1] * grid.shape[2] * 24, 128)

    moved_flat = moved.reshape(cx * 24, 128)

    def row_of(n, y, x, r):
        return ((n * (cy + 2 * LO) + y + LO) * (cx + 2 * LO) + x + LO) * 24 + r

    halves = cx // 16

    def pack(n, c, r):
        y = c * depth + r
        for q in range(2 * halves):
            send_h[n, 0, c, r * 2 * halves + q] = flat[pl.ds(row_of(n, y, 8 * q, 15), 8, stride=24), :]
            send_h[n, 1, c, r * 2 * halves + q] = flat[pl.ds(row_of(n, y, 8 * q, 8), 8, stride=24), :]
        for q in range(halves):
            at = (2 * depth + r) * halves + q
            a = flat[pl.ds(row_of(n, y, 16 * q, 14), 8, stride=24), :]
            b = flat[pl.ds(row_of(n, y, 16 * q + 8, 14), 8, stride=24), :]
            send_h[n, 0, c, at] = jnp.where(low_half, swap(a), b)
            a = flat[pl.ds(row_of(n, y, 16 * q, 9), 8, stride=24), :]
            b = flat[pl.ds(row_of(n, y, 16 * q + 8, 9), 8, stride=24), :]
            send_h[n, 1, c, at] = jnp.where(low_half, a, swap(b))

    def unpack(n, c, r):
        y = c * depth + r
        for q in range(2 * halves):
            flat[pl.ds(row_of(n, y, 8 * q, 7), 8, stride=24), :] = recv_h[n, 0, c, r * 2 * halves + q]
            flat[pl.ds(row_of(n, y, 8 * q, 16), 8, stride=24), :] = recv_h[n, 1, c, r * 2 * halves + q]
        for q in range(halves):
            at = (2 * depth + r) * halves + q
            v = recv_h[n, 0, c, at]
            here = [send_h[n, 1, c, r * 2 * halves + 2 * q + k] for k in range(2)]
            past = [recv_h[n, 0, c, r * 2 * halves + 2 * q + k] for k in range(2)]
            edge, _ = both_ways([
                v,
                jnp.where(low_half, past[0], swap(past[1])), jnp.where(low_half, swap(past[0]), past[1]),
                jnp.where(low_half, here[0], swap(here[1])), jnp.where(low_half, swap(here[0]), here[1]),
                send_h[n, 1, c, at],
            ])
            moved_flat[pl.ds(16 * q * 24 + 7, 8, stride=24), :] = edge
            moved_flat[pl.ds((16 * q + 8) * 24 + 7, 8, stride=24), :] = swap(edge)
            v = recv_h[n, 1, c, at]
            flat[pl.ds(row_of(n, y, 16 * q, 17), 8, stride=24), :] = v
            flat[pl.ds(row_of(n, y, 16 * q + 8, 17), 8, stride=24), :] = swap(v)

    def send_chunk(n, c):
        for copy in h_copies(n, c):
            copy.start()

    def send_y(n, low):
        yu, yd = y_copies(n)
        up = jnp.logical_not(north) if low else north
        pl.when(up & has_yd)(lambda: yu.start())
        pl.when(jnp.logical_not(up) & has_yu)(lambda: yd.start())

    def send_x(n, c):
        xu, xd = x_copies(n, c)
        pl.when(has_xd)(lambda: xu.start())
        pl.when(has_xu)(lambda: xd.start())

    def chunk_at(i):
        return jnp.where(i < 2, i + 1, jnp.where(i == 2, 0, 3))

    send_y(0, True)
    send_y(0, False)

    @pl.loop(0, CHUNKS)
    def _(i):
        c = chunk_at(i)

        @pl.loop(0, depth)
        def _(r):
            pack(0, c, r)

        send_chunk(0, c)
        send_x(0, c)

    @pl.loop(1, total)
    def _(i):
        for c in request((me + i) % total):
            c.start()

    own = (pltpu.make_async_copy(code_ref.at[me], code_in.at[me], loc_sem.at[0]),
           pltpu.make_async_copy(wt_ref.at[me], wt_in.at[me], loc_sem.at[1]))
    for c in own:
        c.start()
    for c in own:
        c.wait()

    drift_x = drift_ref[ha, 0]
    drift_y = drift_ref[ha, 1]

    def y_part(n, first, count):
        @pl.loop(0, cx)
        def _(x):
            line = upwind_line([grid[n, yb + sy * (first + i), x + LO, 8:16, :] for i in range(count + 5)])
            for k in range(count):
                hy[y0 + sy * (first + k), x] = drift_y * line[k]

    def x_part(n, c):
        @pl.loop(0, depth)
        def _(r):
            y = c * depth + r
            line = upwind_line([grid[n, y + LO, xb + sx * i, 8:16, :] for i in range(cx + 5)])
            for k in range(cx):
                hx[y, x0 + sx * k] = drift_x * line[k]

    @pl.loop(0, STEPS)
    def _(n):
        @pl.loop(0, CHUNKS)
        def _(i):
            c = chunk_at(i)
            yu, yd = y_copies(n)
            pl.when((i == 2) & has_yu)(lambda: yu.wait_recv())
            pl.when((i == 2) & has_yd)(lambda: yd.wait_recv())
            y_part(n, depth * jnp.where(north, c, CHUNKS - 1 - c), depth)
            xu, xd = x_copies(n, c)
            pl.when(has_xu)(lambda: xu.wait_recv())
            pl.when(has_xd)(lambda: xd.wait_recv())
            x_part(n, c)
            for copy in h_copies(n, c):
                copy.wait_recv()

            @pl.loop(0, depth)
            def _(r):
                y = c * depth + r
                unpack(n, c, r)
                for x in range(cx):
                    g = [grid[n, y + LO, x + LO, pl.ds(k, 8), :] for k in range(7, 11)]
                    s = [swap(v) for v in g]
                    odd = [jnp.where(low_half, s[k], s[k + 1]) for k in range(3)]
                    forward, negated = both_ways([g[0], odd[0], g[1], odd[1], g[2], odd[2]])
                    forward = swap(forward)
                    moved[x, 8:16, :] = forward
                    forward = jnp.where(low_half, moved[x, 7:15, :], forward)
                    term = jnp.minimum(forward, negated)
                    ham = hx[y, x] + hy[y, x] + (DT / 6.0) * term
                    grid[n + 1, y + LO, x + LO, 8:16, :] = g[1] - jnp.maximum(ham, 0.0)
                pl.when(n < STEPS - 1)(lambda: pack(n + 1, c, r))

            @pl.when(n < STEPS - 1)
            def _():
                send_chunk(n + 1, c)
                send_x(n + 1, c)
                pl.when(i == 2)(lambda: send_y(n + 1, True))
                pl.when(i == 3)(lambda: send_y(n + 1, False))

    @pl.loop(0, cy)
    def _(y):
        for x in range(cx):
            row = x * cy + y
            stage[pl.ds(row, nj, stride=cx * cy), :] = grid[STEPS, y + LO, x + LO, 8:16, :]

    stores = [
        pltpu.make_async_copy(
            stage.at[pl.ds(j * cx * cy, cx * cy)], out_hbm.at[:, pl.ds(128 * j, 128)], out_sem.at[j])
        for j in range(nj)
    ]
    for c in stores:
        c.start()

    @pl.loop(1, total)
    def _(i):
        for c in request_from((me + i) % total):
            c.wait()

    to_s = (pltpu.make_async_copy(code_in, code_s, loc_sem.at[0]),
            pltpu.make_async_copy(wt_in, wt_s, loc_sem.at[1]))
    for c in to_s:
        c.start()
    for c in to_s:
        c.wait()

    ramp = (lax.broadcasted_iota(jnp.int32, (8, 128), 0) * 128
            + lax.broadcasted_iota(jnp.int32, (8, 128), 1))
    hv = nj * 128

    def answer(o, slot_of):
        return pltpu.make_async_remote_copy(
            src_ref=rows.at[o], dst_ref=res_ref.at[slot_of], send_sem=rs_sem.at[o],
            recv_sem=rr_sem.at[slot_of], device_id=device_of(o), device_id_type=MESH)

    @pl.loop(0, total)
    def _(i):
        o = (me + i + 1) % total
        for slot in range(CAP):
            c = jnp.maximum(code_s[o, 0, slot], 0)
            a = c // (cy * hv)
            b = (c // hv) % cy
            at = ramp - c % hv
            hits = [at == off for off in (0, 1, NV, NV + 1)]
            acc = None
            for i1 in range(2):
                for i2 in range(2):
                    w = jnp.zeros((8, 128), jnp.float32)
                    for k in range(4):
                        w = jnp.where(hits[k], wt_s[o, 0, slot * 16 + 8 * i1 + 4 * i2 + k], w)
                    part = w * grid[STEPS, b + i2 + LO, a + i1 + LO, 8:16, :]
                    acc = part if acc is None else acc + part
            rows[o, slot:slot + 1, :] = jnp.sum(acc, axis=0, keepdims=True)
        pl.when(o != me)(lambda: answer(o, me).start())

    mine = pltpu.make_async_copy(rows.at[me], res_ref.at[me], loc_sem.at[2])
    mine.start()
    mine.wait()

    @pl.loop(1, total)
    def _(i):
        o = (me + i) % total
        answer(o, o).wait()

    @pl.loop(0, STEPS)
    def _(n):
        yu, yd = y_copies(n)
        pl.when(has_yd)(lambda: yu.wait_send())
        pl.when(has_yu)(lambda: yd.wait_send())

        @pl.loop(0, CHUNKS)
        def _(c):
            xu, xd = x_copies(n, c)
            pl.when(has_xd)(lambda: xu.wait_send())
            pl.when(has_xu)(lambda: xd.wait_send())
            for copy in h_copies(n, c):
                copy.wait_send()

    for c in stores:
        c.wait()


def drift_table(nha, ch, nj):
    heads = nha * ch
    angle = np.arange(heads, dtype=np.int32).astype(np.float32) * np.float32(6.283185307179586 / heads)
    speed = np.float32(0.5) + np.arange(NV, dtype=np.float32) / np.float32(NV - 1)
    quarter = np.arange(heads) * 4 // heads
    sign_x = np.where((quarter == 0) | (quarter == 3), 1.0, -1.0).astype(np.float32)
    sign_y = np.where(quarter < 2, 1.0, -1.0).astype(np.float32)
    table = np.stack([(sign_x * np.cos(angle))[:, None] * speed, (sign_y * np.sin(angle))[:, None] * speed])
    table = table * np.float32(DT / 6.0)
    return table.reshape(2, nha, nj, 128).transpose(1, 0, 2, 3).astype(np.float32)


def solution(mesh):
    ngx, ngy, nha = (mesh.shape[k] for k in ("gx", "gy", "ha"))
    total = ngx * ngy * nha
    assert nha % 4 == 0

    def local(initial_value, corner, weights):
        cx, cy, chv = initial_value.shape
        nj = chv // 128
        assert nj == 8 and cx % 16 == 0
        table = jnp.asarray(drift_table(nha, chv // NV, nj))
        codes = jnp.pad(corner[0].T, ((0, 0), (0, 128 - CAP))).reshape(total, 1, 128)
        wts = weights[0].transpose(2, 1, 0).reshape(total, CAP * 16)
        wts = jnp.pad(wts, ((0, 0), (0, 128 - CAP * 16))).reshape(total, 1, 128)
        f32, i32 = jnp.float32, jnp.int32
        tiles = cy * (cx // 16) * 3
        dma = pltpu.SemaphoreType.DMA
        vmem = pl.BlockSpec(memory_space=pltpu.VMEM)
        any_ = pl.BlockSpec(memory_space=pl.ANY)
        final, parts = pl.pallas_call(
            functools.partial(kernel, (ngx, ngy, nha, cx, cy, nj)),
            out_shape=(jax.ShapeDtypeStruct((cx * cy, chv), f32),
                       jax.ShapeDtypeStruct((total, CAP, 128), f32)),
            in_specs=[any_, vmem, vmem, vmem],
            out_specs=(any_, vmem),
            scratch_shapes=[
                pltpu.VMEM((STEPS + 1, cy + 2 * LO, cx + 2 * LO, 24, 128), f32),
                pltpu.VMEM((cy, cx, 8, 128), f32),
                pltpu.VMEM((cy, cx, 8, 128), f32),
                pltpu.VMEM((cx, 24, 128), f32),
                pltpu.VMEM((nj * cx * cy, 128), f32),
                pltpu.VMEM((STEPS, 2, CHUNKS, tiles // CHUNKS, 8, 128), f32),
                pltpu.VMEM((STEPS, 2, CHUNKS, tiles // CHUNKS, 8, 128), f32),
                pltpu.VMEM((total, 1, 128), i32),
                pltpu.VMEM((total, 1, 128), f32),
                pltpu.SMEM((total, 1, 128), i32),
                pltpu.SMEM((total, 1, 128), f32),
                pltpu.VMEM((total, CAP, 128), f32),
                dma((nj,)), dma((nj,)), dma((STEPS, 2 + 4 * CHUNKS)), dma((STEPS, 2 + 4 * CHUNKS)),
                dma((total,)), dma((total,)), dma((total,)), dma((total,)),
                dma((total,)), dma((total,)), dma((3,)),
            ],
            compiler_params=pltpu.CompilerParams(
                collective_id=0, has_side_effects=True, vmem_limit_bytes=56 * 1024 * 1024),
        )(initial_value.reshape(cx * cy, chv), codes, wts, table)
        sampled = jnp.sum(parts, axis=2).T[None]
        return (final.reshape(cx, cy, chv), jnp.where(corner >= 0, sampled, 0.0))

    return jax.shard_map(
        local,
        mesh=mesh,
        in_specs=(P("gx", "gy", "ha"), P(("gx", "gy", "ha"), None, None),
                  P(("gx", "gy", "ha"), None, None, None)),
        out_specs=(P("gx", "gy", "ha"), P(("gx", "gy", "ha"), None, None)),
        check_vma=False,
    )
```

```python
import functools

import jax
import jax.numpy as jnp
import numpy as np
from jax import lax
from jax.experimental import pallas as pl
from jax.experimental.pallas import tpu as pltpu
from jax.sharding import PartitionSpec as P

NV = 64
STEPS = 4
CAP = 4
MESH = pl.DeviceIdType.MESH
EPS4 = 4e-6
DT = 0.15
LO, HI = 3, 2
CHUNKS = 4


def smooth(t):
    return (13.0 / 3.0) * (t * t) + EPS4


def weight(v):
    v = pl.reciprocal(v, approx=True)
    return v * v


def terms(cells):
    n = len(cells)
    d = [cells[i + 1] - cells[i] for i in range(n - 1)]
    e = [d[i + 1] - d[i] for i in range(n - 2)]
    t = [e[i + 1] - e[i] for i in range(n - 3)]
    z = [t[i] - t[i + 1] for i in range(n - 4)]
    m = [smooth(v) for v in t]
    e3 = [3.0 * v for v in e]
    return d, e, z, m, e3


def weights_at(i, e, m, e3):
    u1 = e3[i + 1] - e[i]
    u2 = e[i + 1] + e[i + 2]
    u3 = e3[i + 2] - e[i + 3]
    return weight(m[i] + u1 * u1), 6.0 * weight(m[i + 1] + u2 * u2), weight(m[i + 2] + u3 * u3)


def upwind_line(cells):
    d, e, z, m, e3 = terms(cells)
    out = []
    for i in range(len(cells) - 5):
        g1, g2, g3 = weights_at(i, e, m, e3)
        g3 = 3.0 * g3
        num = (z[i] + z[i]) * g1 + z[i + 1] * g3
        lin = 6.0 * d[i + 2] + (e[i + 1] + (e[i + 2] + e[i + 2]))
        out.append(lin + num * pl.reciprocal(g1 + g2 + g3, approx=True))
    return out


def both_ways(cells):
    d, e, z, m, e3 = terms(cells)
    g1, g2, g3 = weights_at(0, e, m, e3)
    c = 6.0 * d[2]
    h1, h3 = 3.0 * g1, 3.0 * g3
    forward = (c + (e[1] + (e[2] + e[2]))
               + ((z[0] + z[0]) * g1 + z[1] * h3) * pl.reciprocal(g1 + g2 + h3, approx=True))
    negated = ((e[2] + (e[1] + e[1])) - c
               + ((z[1] + z[1]) * g3 + z[0] * h1) * pl.reciprocal(h1 + g2 + g3, approx=True))
    return forward, negated


def kernel(sizes, v_hbm, code_ref, wt_ref, drift_ref, corner_ref, out_hbm, res_ref,
           grid, hx, hy, moved, stage, send_h, recv_h, code_in, wt_in, code_s, wt_s, rows, res_in, wt_tile,
           in_sem, out_sem, halo_send, halo_recv, cs_sem, cr_sem, ws_sem, wr_sem, rs_sem, rr_sem, loc_sem):
    ngx, ngy, nha, cx, cy, nj = sizes
    total = ngx * ngy * nha
    gx, gy, ha = lax.axis_index("gx"), lax.axis_index("gy"), lax.axis_index("ha")
    me = (gx * ngy + gy) * nha + ha
    quarter = ha * 4 // nha
    east = (quarter == 0) | (quarter == 3)
    north = quarter < 2
    sx = jnp.where(east, 1, -1)
    sy = jnp.where(north, 1, -1)
    x0 = jnp.where(east, 0, cx - 1)
    y0 = jnp.where(north, 0, cy - 1)
    xb = jnp.where(east, 0, cx + 2 * LO - 1)
    yb = jnp.where(north, 0, cy + 2 * LO - 1)

    def near(forward, a, b, count):
        return pl.ds(jnp.where(forward, a, b), count)

    def up_dst(forward, c):
        return near(forward, 0, c + LO, LO)

    def up_src(forward, c):
        return near(forward, c, LO, LO)

    def down_dst(forward, c):
        return near(forward, c + LO, LO - HI, HI)

    def down_src(forward, c):
        return near(forward, LO, c + LO - HI, HI)


    def device_of(o):
        return (o // (ngy * nha), (o // nha) % ngy, o % nha)

    loads = [
        pltpu.make_async_copy(
            v_hbm.at[:, pl.ds(128 * j, 128)], stage.at[pl.ds(j * cx * cy, cx * cy)], in_sem.at[j])
        for j in range(nj)
    ]
    for c in loads:
        c.start()

    barrier = pltpu.get_barrier_semaphore()

    @pl.loop(1, total)
    def _(i):
        pl.semaphore_signal(barrier, inc=1, device_id=device_of((me + i) % total), device_id_type=MESH)

    tile0 = jnp.zeros((8, 128), jnp.float32)
    x_up = gx - sx
    x_down = gx + sx
    y_up = gy - sy
    y_down = gy + sy
    has_xu = (x_up >= 0) & (x_up < ngx)
    has_xd = (x_down >= 0) & (x_down < ngx)
    has_yu = (y_up >= 0) & (y_up < ngy)
    has_yd = (y_down >= 0) & (y_down < ngy)

    def zero_x(first, count):
        @pl.loop(0, STEPS)
        def _(n):
            @pl.loop(0, cy)
            def _(y):
                for x in range(count):
                    grid[n, y + LO, first + x, 8:16, :] = tile0

    def zero_y(first, count):
        @pl.loop(0, STEPS)
        def _(n):
            @pl.loop(0, cx)
            def _(x):
                for y in range(count):
                    grid[n, first + y, x + LO, 8:16, :] = tile0

    pl.when(jnp.logical_not(has_xu))(lambda: zero_x(jnp.where(east, 0, cx + LO), LO))
    pl.when(jnp.logical_not(has_xd))(lambda: zero_x(jnp.where(east, cx + LO, LO - HI), HI))
    pl.when(jnp.logical_not(has_yu))(lambda: zero_y(jnp.where(north, 0, cy + LO), LO))
    pl.when(jnp.logical_not(has_yd))(lambda: zero_y(jnp.where(north, cy + LO, LO - HI), HI))

    for c in loads:
        c.wait()

    @pl.loop(0, cy)
    def _(y):
        for x in range(cx):
            row = x * cy + y
            grid[0, y + LO, x + LO, 8:16, :] = stage[pl.ds(row, nj, stride=cx * cy), :]

    pl.semaphore_wait(barrier, total - 1)

    def request(o):
        return (
            pltpu.make_async_remote_copy(
                src_ref=code_ref.at[o], dst_ref=code_in.at[me], send_sem=cs_sem.at[o],
                recv_sem=cr_sem.at[me], device_id=device_of(o), device_id_type=MESH),
            pltpu.make_async_remote_copy(
                src_ref=wt_ref.at[o], dst_ref=wt_in.at[me], send_sem=ws_sem.at[o],
                recv_sem=wr_sem.at[me], device_id=device_of(o), device_id_type=MESH),
        )

    def request_from(o):
        return (
            pltpu.make_async_remote_copy(
                src_ref=code_ref.at[o], dst_ref=code_in.at[o], send_sem=cs_sem.at[o],
                recv_sem=cr_sem.at[o], device_id=device_of(o), device_id_type=MESH),
            pltpu.make_async_remote_copy(
                src_ref=wt_ref.at[o], dst_ref=wt_in.at[o], send_sem=ws_sem.at[o],
                recv_sem=wr_sem.at[o], device_id=device_of(o), device_id_type=MESH),
        )

    xs = pl.ds(LO, cx)
    depth = cy // CHUNKS

    def x_copies(n, c):
        g = grid.at[n]
        ys = pl.ds(LO + c * depth, depth)
        up = pltpu.make_async_remote_copy(
            src_ref=g.at[ys, up_src(east, cx), pl.ds(8, 8)], dst_ref=g.at[ys, up_dst(east, cx), pl.ds(8, 8)],
            send_sem=halo_send.at[n, 2 + c], recv_sem=halo_recv.at[n, 2 + c],
            device_id=(x_down, gy, ha), device_id_type=MESH)
        down = pltpu.make_async_remote_copy(
            src_ref=g.at[ys, down_src(east, cx), pl.ds(8, 8)], dst_ref=g.at[ys, down_dst(east, cx), pl.ds(8, 8)],
            send_sem=halo_send.at[n, 2 + CHUNKS + c], recv_sem=halo_recv.at[n, 2 + CHUNKS + c],
            device_id=(x_up, gy, ha), device_id_type=MESH)
        return up, down

    def y_copies(n):
        g = grid.at[n]
        up = pltpu.make_async_remote_copy(
            src_ref=g.at[up_src(north, cy), xs, pl.ds(8, 8)], dst_ref=g.at[up_dst(north, cy), xs, pl.ds(8, 8)],
            send_sem=halo_send.at[n, 0], recv_sem=halo_recv.at[n, 0],
            device_id=(gx, y_down, ha), device_id_type=MESH)
        down = pltpu.make_async_remote_copy(
            src_ref=g.at[down_src(north, cy), xs, pl.ds(8, 8)], dst_ref=g.at[down_dst(north, cy), xs, pl.ds(8, 8)],
            send_sem=halo_send.at[n, 1], recv_sem=halo_recv.at[n, 1],
            device_id=(gx, y_up, ha), device_id_type=MESH)
        return up, down

    def h_copies(n, c):
        return tuple(
            pltpu.make_async_remote_copy(
                src_ref=send_h.at[n, k, c], dst_ref=recv_h.at[n, k, c],
                send_sem=halo_send.at[n, 2 + (2 + k) * CHUNKS + c], recv_sem=halo_recv.at[n, 2 + (2 + k) * CHUNKS + c],
                device_id=(gx, gy, (ha + (1 if k == 0 else nha - 1)) % nha), device_id_type=MESH)
            for k in range(2))

    low_half = lax.broadcasted_iota(jnp.int32, (8, 128), 1) < NV

    def swap(v):
        return pltpu.roll(v, NV, 1)

    flat = grid.reshape(grid.shape[0] * grid.shape[1] * grid.shape[2] * 24, 128)

    moved_flat = moved.reshape(cx * 24, 128)

    def row_of(n, y, x, r):
        return ((n * (cy + 2 * LO) + y + LO) * (cx + 2 * LO) + x + LO) * 24 + r

    halves = cx // 16

    def pack(n, c, r):
        y = c * depth + r
        for q in range(2 * halves):
            send_h[n, 0, c, r * 2 * halves + q] = flat[pl.ds(row_of(n, y, 8 * q, 15), 8, stride=24), :]
            send_h[n, 1, c, r * 2 * halves + q] = flat[pl.ds(row_of(n, y, 8 * q, 8), 8, stride=24), :]
        for q in range(halves):
            at = (2 * depth + r) * halves + q
            a = flat[pl.ds(row_of(n, y, 16 * q, 14), 8, stride=24), :]
            b = flat[pl.ds(row_of(n, y, 16 * q + 8, 14), 8, stride=24), :]
            send_h[n, 0, c, at] = jnp.where(low_half, swap(a), b)
            a = flat[pl.ds(row_of(n, y, 16 * q, 9), 8, stride=24), :]
            b = flat[pl.ds(row_of(n, y, 16 * q + 8, 9), 8, stride=24), :]
            send_h[n, 1, c, at] = jnp.where(low_half, a, swap(b))

    def unpack(n, c, r):
        y = c * depth + r
        for q in range(2 * halves):
            flat[pl.ds(row_of(n, y, 8 * q, 7), 8, stride=24), :] = recv_h[n, 0, c, r * 2 * halves + q]
            flat[pl.ds(row_of(n, y, 8 * q, 16), 8, stride=24), :] = recv_h[n, 1, c, r * 2 * halves + q]
        for q in range(halves):
            at = (2 * depth + r) * halves + q
            v = recv_h[n, 0, c, at]
            here = [send_h[n, 1, c, r * 2 * halves + 2 * q + k] for k in range(2)]
            past = [recv_h[n, 0, c, r * 2 * halves + 2 * q + k] for k in range(2)]
            edge, _ = both_ways([
                v,
                jnp.where(low_half, past[0], swap(past[1])), jnp.where(low_half, swap(past[0]), past[1]),
                jnp.where(low_half, here[0], swap(here[1])), jnp.where(low_half, swap(here[0]), here[1]),
                send_h[n, 1, c, at],
            ])
            moved_flat[pl.ds(16 * q * 24 + 7, 8, stride=24), :] = edge
            moved_flat[pl.ds((16 * q + 8) * 24 + 7, 8, stride=24), :] = swap(edge)
            v = recv_h[n, 1, c, at]
            flat[pl.ds(row_of(n, y, 16 * q, 17), 8, stride=24), :] = v
            flat[pl.ds(row_of(n, y, 16 * q + 8, 17), 8, stride=24), :] = swap(v)

    def send_chunk(n, c):
        for copy in h_copies(n, c):
            copy.start()

    def send_y(n, low):
        yu, yd = y_copies(n)
        up = jnp.logical_not(north) if low else north
        pl.when(up & has_yd)(lambda: yu.start())
        pl.when(jnp.logical_not(up) & has_yu)(lambda: yd.start())

    def send_x(n, c):
        xu, xd = x_copies(n, c)
        pl.when(has_xd)(lambda: xu.start())
        pl.when(has_xu)(lambda: xd.start())

    def chunk_at(i):
        return jnp.where(i < 2, i + 1, jnp.where(i == 2, 0, 3))

    send_y(0, True)
    send_y(0, False)

    @pl.loop(0, CHUNKS)
    def _(i):
        c = chunk_at(i)

        @pl.loop(0, depth)
        def _(r):
            pack(0, c, r)

        send_chunk(0, c)
        send_x(0, c)

    @pl.loop(1, total)
    def _(i):
        for c in request((me + i) % total):
            c.start()

    own = (pltpu.make_async_copy(code_ref.at[me], code_in.at[me], loc_sem.at[0]),
           pltpu.make_async_copy(wt_ref.at[me], wt_in.at[me], loc_sem.at[1]))
    for c in own:
        c.start()
    for c in own:
        c.wait()

    drift_x = drift_ref[ha, 0]
    drift_y = drift_ref[ha, 1]

    def y_part(n, first, count):
        @pl.loop(0, cx)
        def _(x):
            line = upwind_line([grid[n, yb + sy * (first + i), x + LO, 8:16, :] for i in range(count + 5)])
            for k in range(count):
                hy[y0 + sy * (first + k), x] = drift_y * line[k]

    def x_part(n, c):
        @pl.loop(0, depth)
        def _(r):
            y = c * depth + r
            line = upwind_line([grid[n, y + LO, xb + sx * i, 8:16, :] for i in range(cx + 5)])
            for k in range(cx):
                hx[y, x0 + sx * k] = drift_x * line[k]

    ramp = (lax.broadcasted_iota(jnp.int32, (8, 128), 0) * 128
            + lax.broadcasted_iota(jnp.int32, (8, 128), 1))
    hv = nj * 128

    def get_requests():
        @pl.loop(1, total)
        def _(i):
            for c in request_from((me + i) % total):
                c.wait()

        to_s = (pltpu.make_async_copy(code_in, code_s, loc_sem.at[0]),
                pltpu.make_async_copy(wt_in, wt_s, loc_sem.at[1]))
        for c in to_s:
            c.start()
        for c in to_s:
            c.wait()

    def weight_tiles(n):
        @pl.loop(0, total // STEPS)
        def _(q):
            o = n * (total // STEPS) + q
            for slot in range(CAP):
                at = ramp - lax.rem(jnp.maximum(code_s[o, 0, slot], 0), hv)
                hits = [at == off for off in (0, 1, NV, NV + 1)]
                for m in range(4):
                    w = jnp.zeros((8, 128), jnp.float32)
                    for k in range(4):
                        w = jnp.where(hits[k], wt_s[o, 0, slot * 16 + 4 * m + k], w)
                    wt_tile[o * CAP + slot, m] = w

    @pl.loop(0, STEPS)
    def _(n):
        @pl.loop(0, CHUNKS)
        def _(i):
            c = chunk_at(i)
            yu, yd = y_copies(n)
            pl.when((i == 2) & has_yu)(lambda: yu.wait_recv())
            pl.when((i == 2) & has_yd)(lambda: yd.wait_recv())
            y_part(n, depth * jnp.where(north, c, CHUNKS - 1 - c), depth)
            xu, xd = x_copies(n, c)
            pl.when(has_xu)(lambda: xu.wait_recv())
            pl.when(has_xd)(lambda: xd.wait_recv())
            x_part(n, c)
            for copy in h_copies(n, c):
                copy.wait_recv()

            @pl.loop(0, depth)
            def _(r):
                y = c * depth + r
                unpack(n, c, r)
                for x in range(cx):
                    g = [grid[n, y + LO, x + LO, pl.ds(k, 8), :] for k in range(7, 11)]
                    s = [swap(v) for v in g]
                    odd = [jnp.where(low_half, s[k], s[k + 1]) for k in range(3)]
                    forward, negated = both_ways([g[0], odd[0], g[1], odd[1], g[2], odd[2]])
                    forward = swap(forward)
                    moved[x, 8:16, :] = forward
                    forward = jnp.where(low_half, moved[x, 7:15, :], forward)
                    term = jnp.minimum(forward, negated)
                    ham = hx[y, x] + hy[y, x] + (DT / 6.0) * term
                    grid[n + 1, y + LO, x + LO, 8:16, :] = g[1] - jnp.maximum(ham, 0.0)
                pl.when(n < STEPS - 1)(lambda: pack(n + 1, c, r))

            @pl.when(n == STEPS - 1)
            def _():
                @pl.loop(0, depth)
                def _(r):
                    y = c * depth + r
                    for x in range(cx):
                        stage[pl.ds(x * cy + y, nj, stride=cx * cy), :] = grid[STEPS, y + LO, x + LO, 8:16, :]

            @pl.when(n < STEPS - 1)
            def _():
                send_chunk(n + 1, c)
                send_x(n + 1, c)
                pl.when(i == 2)(lambda: send_y(n + 1, True))
                pl.when(i == 3)(lambda: send_y(n + 1, False))

            pl.when((n == 0) & (i == 2))(get_requests)
            pl.when(i == 2)(lambda: weight_tiles(n))

    stores = [
        pltpu.make_async_copy(
            stage.at[pl.ds(j * cx * cy, cx * cy)], out_hbm.at[:, pl.ds(128 * j, 128)], out_sem.at[j])
        for j in range(nj)
    ]
    for c in stores:
        c.start()

    def answer(o, slot_of):
        return pltpu.make_async_remote_copy(
            src_ref=rows.at[o], dst_ref=res_in.at[slot_of], send_sem=rs_sem.at[o],
            recv_sem=rr_sem.at[slot_of], device_id=device_of(o), device_id_type=MESH)

    @pl.loop(0, total)
    def _(i):
        o = (me + i + 1) % total
        for slot in range(CAP):
            c = jnp.maximum(code_s[o, 0, slot], 0)
            a = lax.div(c, cy * hv)
            b = lax.rem(lax.div(c, hv), cy)
            part = [wt_tile[o * CAP + slot, 2 * i1 + i2] * grid[STEPS, b + i2 + LO, a + i1 + LO, 8:16, :]
                    for i1 in range(2) for i2 in range(2)]
            acc = (part[0] + part[1]) + (part[2] + part[3])
            rows[o, slot:slot + 1, :] = jnp.sum(acc, axis=0, keepdims=True)
        pl.when(o != me)(lambda: answer(o, me).start())

    mine = pltpu.make_async_copy(rows.at[me], res_in.at[me], loc_sem.at[2])
    mine.start()
    mine.wait()

    @pl.loop(1, total)
    def _(i):
        o = (me + i) % total
        answer(o, o).wait()

    for slot in range(CAP):
        sums = jnp.sum(res_in[:, slot, :].T, axis=0, keepdims=True)
        res_ref[slot:slot + 1, :] = jnp.where(corner_ref[slot:slot + 1, :] >= 0, sums, 0.0)

    @pl.loop(0, STEPS)
    def _(n):
        yu, yd = y_copies(n)
        pl.when(has_yd)(lambda: yu.wait_send())
        pl.when(has_yu)(lambda: yd.wait_send())

        @pl.loop(0, CHUNKS)
        def _(c):
            xu, xd = x_copies(n, c)
            pl.when(has_xd)(lambda: xu.wait_send())
            pl.when(has_xu)(lambda: xd.wait_send())
            for copy in h_copies(n, c):
                copy.wait_send()

    for c in stores:
        c.wait()


def drift_table(nha, ch, nj):
    heads = nha * ch
    angle = np.arange(heads, dtype=np.int32).astype(np.float32) * np.float32(6.283185307179586 / heads)
    speed = np.float32(0.5) + np.arange(NV, dtype=np.float32) / np.float32(NV - 1)
    quarter = np.arange(heads) * 4 // heads
    sign_x = np.where((quarter == 0) | (quarter == 3), 1.0, -1.0).astype(np.float32)
    sign_y = np.where(quarter < 2, 1.0, -1.0).astype(np.float32)
    table = np.stack([(sign_x * np.cos(angle))[:, None] * speed, (sign_y * np.sin(angle))[:, None] * speed])
    table = table * np.float32(DT / 6.0)
    return table.reshape(2, nha, nj, 128).transpose(1, 0, 2, 3).astype(np.float32)


def solution(mesh):
    ngx, ngy, nha = (mesh.shape[k] for k in ("gx", "gy", "ha"))
    total = ngx * ngy * nha
    assert nha % 4 == 0 and total % STEPS == 0

    def local(initial_value, corner, weights):
        cx, cy, chv = initial_value.shape
        nj = chv // 128
        assert nj == 8 and cx % 16 == 0
        table = jnp.asarray(drift_table(nha, chv // NV, nj))
        codes = jnp.pad(corner[0].T, ((0, 0), (0, 128 - CAP))).reshape(total, 1, 128)
        wts = weights[0].transpose(2, 1, 0).reshape(total, CAP * 16)
        wts = jnp.pad(wts, ((0, 0), (0, 128 - CAP * 16))).reshape(total, 1, 128)
        f32, i32 = jnp.float32, jnp.int32
        tiles = cy * (cx // 16) * 3
        dma = pltpu.SemaphoreType.DMA
        vmem = pl.BlockSpec(memory_space=pltpu.VMEM)
        any_ = pl.BlockSpec(memory_space=pl.ANY)
        final, samples = pl.pallas_call(
            functools.partial(kernel, (ngx, ngy, nha, cx, cy, nj)),
            out_shape=(jax.ShapeDtypeStruct((cx * cy, chv), f32),
                       jax.ShapeDtypeStruct((CAP, total), f32)),
            in_specs=[any_, vmem, vmem, vmem, vmem],
            out_specs=(any_, vmem),
            scratch_shapes=[
                pltpu.VMEM((STEPS + 1, cy + 2 * LO, cx + 2 * LO, 24, 128), f32),
                pltpu.VMEM((cy, cx, 8, 128), f32),
                pltpu.VMEM((cy, cx, 8, 128), f32),
                pltpu.VMEM((cx, 24, 128), f32),
                pltpu.VMEM((nj * cx * cy, 128), f32),
                pltpu.VMEM((STEPS, 2, CHUNKS, tiles // CHUNKS, 8, 128), f32),
                pltpu.VMEM((STEPS, 2, CHUNKS, tiles // CHUNKS, 8, 128), f32),
                pltpu.VMEM((total, 1, 128), i32),
                pltpu.VMEM((total, 1, 128), f32),
                pltpu.SMEM((total, 1, 128), i32),
                pltpu.SMEM((total, 1, 128), f32),
                pltpu.VMEM((total, CAP, 128), f32),
                pltpu.VMEM((total, CAP, 128), f32),
                pltpu.VMEM((total * CAP, 4, 8, 128), f32),
                dma((nj,)), dma((nj,)), dma((STEPS, 2 + 4 * CHUNKS)), dma((STEPS, 2 + 4 * CHUNKS)),
                dma((total,)), dma((total,)), dma((total,)), dma((total,)),
                dma((total,)), dma((total,)), dma((3,)),
            ],
            compiler_params=pltpu.CompilerParams(
                collective_id=0, has_side_effects=True, vmem_limit_bytes=56 * 1024 * 1024),
        )(initial_value.reshape(cx * cy, chv), codes, wts, table, corner[0])
        return (final.reshape(cx, cy, chv), samples[None])

    return jax.shard_map(
        local,
        mesh=mesh,
        in_specs=(P("gx", "gy", "ha"), P(("gx", "gy", "ha"), None, None),
                  P(("gx", "gy", "ha"), None, None, None)),
        out_specs=(P("gx", "gy", "ha"), P(("gx", "gy", "ha"), None, None)),
        check_vma=False,
    )
```

```python
import functools

import jax
import jax.numpy as jnp
import numpy as np
from jax import lax
from jax.experimental import pallas as pl
from jax.experimental.pallas import tpu as pltpu
from jax.sharding import PartitionSpec as P

NV = 64
STEPS = 4
CAP = 4
MESH = pl.DeviceIdType.MESH
EPS4 = 4e-6
DT = 0.15
LO, HI = 3, 2
CHUNKS = 4


def smooth(t):
    return (13.0 / 3.0) * (t * t) + EPS4


def square(v):
    return v * v


def terms(cells):
    n = len(cells)
    d = [cells[i + 1] - cells[i] for i in range(n - 1)]
    e = [d[i + 1] - d[i] for i in range(n - 2)]
    t = [e[i + 1] - e[i] for i in range(n - 3)]
    z = [t[i] - t[i + 1] for i in range(n - 4)]
    m = [smooth(v) for v in t]
    e3 = [3.0 * v for v in e]
    return d, e, z, m, e3


def products_at(i, e, m, e3):
    u1 = e3[i + 1] - e[i]
    u2 = e[i + 1] + e[i + 2]
    u3 = e3[i + 2] - e[i + 3]
    s1, s2, s3 = square(m[i] + u1 * u1), square(m[i + 1] + u2 * u2), square(m[i + 2] + u3 * u3)
    return s2 * s3, 6.0 * (s1 * s3), s1 * s2


def upwind_line(cells):
    d, e, z, m, e3 = terms(cells)
    out = []
    for i in range(len(cells) - 5):
        g1, g2, g3 = products_at(i, e, m, e3)
        g3 = 3.0 * g3
        num = (z[i] + z[i]) * g1 + z[i + 1] * g3
        lin = 6.0 * d[i + 2] + (e[i + 1] + (e[i + 2] + e[i + 2]))
        out.append(lin + num * pl.reciprocal(g1 + g2 + g3, approx=True))
    return out


def both_ways(cells):
    d, e, z, m, e3 = terms(cells)
    g1, g2, g3 = products_at(0, e, m, e3)
    c = 6.0 * d[2]
    h1, h3 = 3.0 * g1, 3.0 * g3
    forward = (c + (e[1] + (e[2] + e[2]))
               + ((z[0] + z[0]) * g1 + z[1] * h3) * pl.reciprocal(g1 + g2 + h3, approx=True))
    negated = ((e[2] + (e[1] + e[1])) - c
               + ((z[1] + z[1]) * g3 + z[0] * h1) * pl.reciprocal(h1 + g2 + g3, approx=True))
    return forward, negated


def kernel(sizes, v_hbm, code_ref, wt_ref, drift_ref, corner_ref, out_hbm, res_ref,
           grid, hx, hy, moved, stage, send_h, recv_h, code_in, wt_in, code_s, wt_s, rows, res_in, wt_tile,
           in_sem, out_sem, halo_send, halo_recv, cs_sem, cr_sem, ws_sem, wr_sem, rs_sem, rr_sem, loc_sem):
    ngx, ngy, nha, cx, cy, nj = sizes
    total = ngx * ngy * nha
    gx, gy, ha = lax.axis_index("gx"), lax.axis_index("gy"), lax.axis_index("ha")
    me = (gx * ngy + gy) * nha + ha
    quarter = ha * 4 // nha
    east = (quarter == 0) | (quarter == 3)
    north = quarter < 2
    sx = jnp.where(east, 1, -1)
    sy = jnp.where(north, 1, -1)
    x0 = jnp.where(east, 0, cx - 1)
    y0 = jnp.where(north, 0, cy - 1)
    xb = jnp.where(east, 0, cx + 2 * LO - 1)
    yb = jnp.where(north, 0, cy + 2 * LO - 1)

    def near(forward, a, b, count):
        return pl.ds(jnp.where(forward, a, b), count)

    def up_dst(forward, c):
        return near(forward, 0, c + LO, LO)

    def up_src(forward, c):
        return near(forward, c, LO, LO)

    def down_dst(forward, c):
        return near(forward, c + LO, LO - HI, HI)

    def down_src(forward, c):
        return near(forward, LO, c + LO - HI, HI)


    def device_of(o):
        return (o // (ngy * nha), (o // nha) % ngy, o % nha)

    loads = [
        pltpu.make_async_copy(
            v_hbm.at[:, pl.ds(128 * j, 128)], stage.at[pl.ds(j * cx * cy, cx * cy)], in_sem.at[j])
        for j in range(nj)
    ]
    for c in loads:
        c.start()

    barrier = pltpu.get_barrier_semaphore()

    @pl.loop(1, total)
    def _(i):
        pl.semaphore_signal(barrier, inc=1, device_id=device_of((me + i) % total), device_id_type=MESH)

    tile0 = jnp.zeros((8, 128), jnp.float32)
    x_up = gx - sx
    x_down = gx + sx
    y_up = gy - sy
    y_down = gy + sy
    has_xu = (x_up >= 0) & (x_up < ngx)
    has_xd = (x_down >= 0) & (x_down < ngx)
    has_yu = (y_up >= 0) & (y_up < ngy)
    has_yd = (y_down >= 0) & (y_down < ngy)

    def zero_x(first, count):
        @pl.loop(0, STEPS)
        def _(n):
            @pl.loop(0, cy)
            def _(y):
                for x in range(count):
                    grid[n, y + LO, first + x, 8:16, :] = tile0

    def zero_y(first, count):
        @pl.loop(0, STEPS)
        def _(n):
            @pl.loop(0, cx)
            def _(x):
                for y in range(count):
                    grid[n, first + y, x + LO, 8:16, :] = tile0

    pl.when(jnp.logical_not(has_xu))(lambda: zero_x(jnp.where(east, 0, cx + LO), LO))
    pl.when(jnp.logical_not(has_xd))(lambda: zero_x(jnp.where(east, cx + LO, LO - HI), HI))
    pl.when(jnp.logical_not(has_yu))(lambda: zero_y(jnp.where(north, 0, cy + LO), LO))
    pl.when(jnp.logical_not(has_yd))(lambda: zero_y(jnp.where(north, cy + LO, LO - HI), HI))

    for c in loads:
        c.wait()

    @pl.loop(0, cy)
    def _(y):
        for x in range(cx):
            row = x * cy + y
            grid[0, y + LO, x + LO, 8:16, :] = stage[pl.ds(row, nj, stride=cx * cy), :]

    pl.semaphore_wait(barrier, total - 1)

    def request(o):
        return (
            pltpu.make_async_remote_copy(
                src_ref=code_ref.at[o], dst_ref=code_in.at[me], send_sem=cs_sem.at[o],
                recv_sem=cr_sem.at[me], device_id=device_of(o), device_id_type=MESH),
            pltpu.make_async_remote_copy(
                src_ref=wt_ref.at[o], dst_ref=wt_in.at[me], send_sem=ws_sem.at[o],
                recv_sem=wr_sem.at[me], device_id=device_of(o), device_id_type=MESH),
        )

    def request_from(o):
        return (
            pltpu.make_async_remote_copy(
                src_ref=code_ref.at[o], dst_ref=code_in.at[o], send_sem=cs_sem.at[o],
                recv_sem=cr_sem.at[o], device_id=device_of(o), device_id_type=MESH),
            pltpu.make_async_remote_copy(
                src_ref=wt_ref.at[o], dst_ref=wt_in.at[o], send_sem=ws_sem.at[o],
                recv_sem=wr_sem.at[o], device_id=device_of(o), device_id_type=MESH),
        )

    xs = pl.ds(LO, cx)
    depth = cy // CHUNKS

    def x_copies(n, c):
        g = grid.at[n]
        ys = pl.ds(LO + c * depth, depth)
        up = pltpu.make_async_remote_copy(
            src_ref=g.at[ys, up_src(east, cx), pl.ds(8, 8)], dst_ref=g.at[ys, up_dst(east, cx), pl.ds(8, 8)],
            send_sem=halo_send.at[n, 2 + c], recv_sem=halo_recv.at[n, 2 + c],
            device_id=(x_down, gy, ha), device_id_type=MESH)
        down = pltpu.make_async_remote_copy(
            src_ref=g.at[ys, down_src(east, cx), pl.ds(8, 8)], dst_ref=g.at[ys, down_dst(east, cx), pl.ds(8, 8)],
            send_sem=halo_send.at[n, 2 + CHUNKS + c], recv_sem=halo_recv.at[n, 2 + CHUNKS + c],
            device_id=(x_up, gy, ha), device_id_type=MESH)
        return up, down

    def y_copies(n):
        g = grid.at[n]
        up = pltpu.make_async_remote_copy(
            src_ref=g.at[up_src(north, cy), xs, pl.ds(8, 8)], dst_ref=g.at[up_dst(north, cy), xs, pl.ds(8, 8)],
            send_sem=halo_send.at[n, 0], recv_sem=halo_recv.at[n, 0],
            device_id=(gx, y_down, ha), device_id_type=MESH)
        down = pltpu.make_async_remote_copy(
            src_ref=g.at[down_src(north, cy), xs, pl.ds(8, 8)], dst_ref=g.at[down_dst(north, cy), xs, pl.ds(8, 8)],
            send_sem=halo_send.at[n, 1], recv_sem=halo_recv.at[n, 1],
            device_id=(gx, y_up, ha), device_id_type=MESH)
        return up, down

    def h_copies(n, c):
        return tuple(
            pltpu.make_async_remote_copy(
                src_ref=send_h.at[n, k, c], dst_ref=recv_h.at[n, k, c],
                send_sem=halo_send.at[n, 2 + (2 + k) * CHUNKS + c], recv_sem=halo_recv.at[n, 2 + (2 + k) * CHUNKS + c],
                device_id=(gx, gy, (ha + (1 if k == 0 else nha - 1)) % nha), device_id_type=MESH)
            for k in range(2))

    low_half = lax.broadcasted_iota(jnp.int32, (8, 128), 1) < NV

    def swap(v):
        return pltpu.roll(v, NV, 1)

    flat = grid.reshape(grid.shape[0] * grid.shape[1] * grid.shape[2] * 24, 128)

    moved_flat = moved.reshape(cx * 24, 128)

    def row_of(n, y, x, r):
        return ((n * (cy + 2 * LO) + y + LO) * (cx + 2 * LO) + x + LO) * 24 + r

    halves = cx // 16

    def pack(n, c, r):
        y = c * depth + r
        for q in range(2 * halves):
            send_h[n, 0, c, r * 2 * halves + q] = flat[pl.ds(row_of(n, y, 8 * q, 15), 8, stride=24), :]
            send_h[n, 1, c, r * 2 * halves + q] = flat[pl.ds(row_of(n, y, 8 * q, 8), 8, stride=24), :]
        for q in range(halves):
            at = (2 * depth + r) * halves + q
            a = flat[pl.ds(row_of(n, y, 16 * q, 14), 8, stride=24), :]
            b = flat[pl.ds(row_of(n, y, 16 * q + 8, 14), 8, stride=24), :]
            send_h[n, 0, c, at] = jnp.where(low_half, swap(a), b)
            a = flat[pl.ds(row_of(n, y, 16 * q, 9), 8, stride=24), :]
            b = flat[pl.ds(row_of(n, y, 16 * q + 8, 9), 8, stride=24), :]
            send_h[n, 1, c, at] = jnp.where(low_half, a, swap(b))

    def unpack(n, c, r):
        y = c * depth + r
        for q in range(2 * halves):
            flat[pl.ds(row_of(n, y, 8 * q, 7), 8, stride=24), :] = recv_h[n, 0, c, r * 2 * halves + q]
            flat[pl.ds(row_of(n, y, 8 * q, 16), 8, stride=24), :] = recv_h[n, 1, c, r * 2 * halves + q]
        for q in range(halves):
            at = (2 * depth + r) * halves + q
            v = recv_h[n, 0, c, at]
            here = [send_h[n, 1, c, r * 2 * halves + 2 * q + k] for k in range(2)]
            past = [recv_h[n, 0, c, r * 2 * halves + 2 * q + k] for k in range(2)]
            edge, _ = both_ways([
                v,
                jnp.where(low_half, past[0], swap(past[1])), jnp.where(low_half, swap(past[0]), past[1]),
                jnp.where(low_half, here[0], swap(here[1])), jnp.where(low_half, swap(here[0]), here[1]),
                send_h[n, 1, c, at],
            ])
            moved_flat[pl.ds(16 * q * 24 + 7, 8, stride=24), :] = edge
            moved_flat[pl.ds((16 * q + 8) * 24 + 7, 8, stride=24), :] = swap(edge)
            v = recv_h[n, 1, c, at]
            flat[pl.ds(row_of(n, y, 16 * q, 17), 8, stride=24), :] = v
            flat[pl.ds(row_of(n, y, 16 * q + 8, 17), 8, stride=24), :] = swap(v)

    def send_chunk(n, c):
        for copy in h_copies(n, c):
            copy.start()

    def send_y(n, low):
        yu, yd = y_copies(n)
        up = jnp.logical_not(north) if low else north
        pl.when(up & has_yd)(lambda: yu.start())
        pl.when(jnp.logical_not(up) & has_yu)(lambda: yd.start())

    def send_x(n, c):
        xu, xd = x_copies(n, c)
        pl.when(has_xd)(lambda: xu.start())
        pl.when(has_xu)(lambda: xd.start())

    def chunk_at(i):
        return jnp.where(i < 2, i + 1, jnp.where(i == 2, 0, 3))

    send_y(0, True)
    send_y(0, False)

    @pl.loop(0, CHUNKS)
    def _(i):
        c = chunk_at(i)

        @pl.loop(0, depth)
        def _(r):
            pack(0, c, r)

        send_chunk(0, c)
        send_x(0, c)

    @pl.loop(1, total)
    def _(i):
        for c in request((me + i) % total):
            c.start()

    own = (pltpu.make_async_copy(code_ref.at[me], code_in.at[me], loc_sem.at[0]),
           pltpu.make_async_copy(wt_ref.at[me], wt_in.at[me], loc_sem.at[1]))
    for c in own:
        c.start()
    for c in own:
        c.wait()

    drift_x = drift_ref[ha, 0]
    drift_y = drift_ref[ha, 1]

    def y_part(n, first, count):
        @pl.loop(0, cx // 4)
        def _(q):
            for p in range(4):
                x = 4 * q + p
                line = upwind_line([grid[n, yb + sy * (first + i), x + LO, 8:16, :] for i in range(count + 5)])
                for k in range(count):
                    hy[y0 + sy * (first + k), x] = drift_y * line[k]

    def x_part(n, c):
        @pl.loop(0, depth)
        def _(r):
            y = c * depth + r
            line = upwind_line([grid[n, y + LO, xb + sx * i, 8:16, :] for i in range(cx + 5)])
            for k in range(cx):
                hx[y, x0 + sx * k] = drift_x * line[k]

    ramp = (lax.broadcasted_iota(jnp.int32, (8, 128), 0) * 128
            + lax.broadcasted_iota(jnp.int32, (8, 128), 1))
    hv = nj * 128

    def get_requests():
        @pl.loop(1, total)
        def _(i):
            for c in request_from((me + i) % total):
                c.wait()

        to_s = (pltpu.make_async_copy(code_in, code_s, loc_sem.at[0]),
                pltpu.make_async_copy(wt_in, wt_s, loc_sem.at[1]))
        for c in to_s:
            c.start()
        for c in to_s:
            c.wait()

    def weight_tiles(n):
        @pl.loop(0, total // STEPS)
        def _(q):
            o = n * (total // STEPS) + q
            for slot in range(CAP):
                at = ramp - lax.rem(jnp.maximum(code_s[o, 0, slot], 0), hv)
                hits = [at == off for off in (0, 1, NV, NV + 1)]
                for m in range(4):
                    w = jnp.zeros((8, 128), jnp.float32)
                    for k in range(4):
                        w = jnp.where(hits[k], wt_s[o, 0, slot * 16 + 4 * m + k], w)
                    wt_tile[o * CAP + slot, m] = w

    @pl.loop(0, STEPS)
    def _(n):
        @pl.loop(0, CHUNKS)
        def _(i):
            c = chunk_at(i)
            yu, yd = y_copies(n)
            pl.when((i == 2) & has_yu)(lambda: yu.wait_recv())
            pl.when((i == 2) & has_yd)(lambda: yd.wait_recv())
            y_part(n, depth * jnp.where(north, c, CHUNKS - 1 - c), depth)
            xu, xd = x_copies(n, c)
            pl.when(has_xu)(lambda: xu.wait_recv())
            pl.when(has_xd)(lambda: xd.wait_recv())
            x_part(n, c)
            for copy in h_copies(n, c):
                copy.wait_recv()

            @pl.loop(0, depth)
            def _(r):
                y = c * depth + r
                unpack(n, c, r)
                for x in range(cx):
                    g = [grid[n, y + LO, x + LO, pl.ds(k, 8), :] for k in range(7, 11)]
                    s = [swap(v) for v in g]
                    odd = [jnp.where(low_half, s[k], s[k + 1]) for k in range(3)]
                    forward, negated = both_ways([g[0], odd[0], g[1], odd[1], g[2], odd[2]])
                    forward = swap(forward)
                    moved[x, 8:16, :] = forward
                    forward = jnp.where(low_half, moved[x, 7:15, :], forward)
                    term = jnp.minimum(forward, negated)
                    ham = hx[y, x] + hy[y, x] + (DT / 6.0) * term
                    grid[n + 1, y + LO, x + LO, 8:16, :] = g[1] - jnp.maximum(ham, 0.0)
                pl.when(n < STEPS - 1)(lambda: pack(n + 1, c, r))

            @pl.when(n == STEPS - 1)
            def _():
                @pl.loop(0, depth)
                def _(r):
                    y = c * depth + r
                    for x in range(cx):
                        stage[pl.ds(x * cy + y, nj, stride=cx * cy), :] = grid[STEPS, y + LO, x + LO, 8:16, :]

            @pl.when(n < STEPS - 1)
            def _():
                send_chunk(n + 1, c)
                send_x(n + 1, c)
                pl.when(i == 2)(lambda: send_y(n + 1, True))
                pl.when(i == 3)(lambda: send_y(n + 1, False))

            pl.when((n == 0) & (i == 2))(get_requests)
            pl.when(i == 2)(lambda: weight_tiles(n))

    stores = [
        pltpu.make_async_copy(
            stage.at[pl.ds(j * cx * cy, cx * cy)], out_hbm.at[:, pl.ds(128 * j, 128)], out_sem.at[j])
        for j in range(nj)
    ]
    for c in stores:
        c.start()

    def answer(o, slot_of):
        return pltpu.make_async_remote_copy(
            src_ref=rows.at[o], dst_ref=res_in.at[slot_of], send_sem=rs_sem.at[o],
            recv_sem=rr_sem.at[slot_of], device_id=device_of(o), device_id_type=MESH)

    @pl.loop(0, total)
    def _(i):
        o = (me + i + 1) % total
        for slot in range(CAP):
            c = jnp.maximum(code_s[o, 0, slot], 0)
            a = lax.div(c, cy * hv)
            b = lax.rem(lax.div(c, hv), cy)
            part = [wt_tile[o * CAP + slot, 2 * i1 + i2] * grid[STEPS, b + i2 + LO, a + i1 + LO, 8:16, :]
                    for i1 in range(2) for i2 in range(2)]
            acc = (part[0] + part[1]) + (part[2] + part[3])
            rows[o, slot:slot + 1, :] = jnp.sum(acc, axis=0, keepdims=True)
        pl.when(o != me)(lambda: answer(o, me).start())

    mine = pltpu.make_async_copy(rows.at[me], res_in.at[me], loc_sem.at[2])
    mine.start()
    mine.wait()

    @pl.loop(1, total)
    def _(i):
        o = (me + i) % total
        answer(o, o).wait()

    for slot in range(CAP):
        sums = jnp.sum(res_in[:, slot, :].T, axis=0, keepdims=True)
        res_ref[slot:slot + 1, :] = jnp.where(corner_ref[slot:slot + 1, :] >= 0, sums, 0.0)

    @pl.loop(0, STEPS)
    def _(n):
        yu, yd = y_copies(n)
        pl.when(has_yd)(lambda: yu.wait_send())
        pl.when(has_yu)(lambda: yd.wait_send())

        @pl.loop(0, CHUNKS)
        def _(c):
            xu, xd = x_copies(n, c)
            pl.when(has_xd)(lambda: xu.wait_send())
            pl.when(has_xu)(lambda: xd.wait_send())
            for copy in h_copies(n, c):
                copy.wait_send()

    for c in stores:
        c.wait()


def drift_table(nha, ch, nj):
    heads = nha * ch
    angle = np.arange(heads, dtype=np.int32).astype(np.float32) * np.float32(6.283185307179586 / heads)
    speed = np.float32(0.5) + np.arange(NV, dtype=np.float32) / np.float32(NV - 1)
    quarter = np.arange(heads) * 4 // heads
    sign_x = np.where((quarter == 0) | (quarter == 3), 1.0, -1.0).astype(np.float32)
    sign_y = np.where(quarter < 2, 1.0, -1.0).astype(np.float32)
    table = np.stack([(sign_x * np.cos(angle))[:, None] * speed, (sign_y * np.sin(angle))[:, None] * speed])
    table = table * np.float32(DT / 6.0)
    return table.reshape(2, nha, nj, 128).transpose(1, 0, 2, 3).astype(np.float32)


def solution(mesh):
    ngx, ngy, nha = (mesh.shape[k] for k in ("gx", "gy", "ha"))
    total = ngx * ngy * nha
    assert nha % 4 == 0 and total % STEPS == 0

    def local(initial_value, corner, weights):
        cx, cy, chv = initial_value.shape
        nj = chv // 128
        assert nj == 8 and cx % 16 == 0
        table = jnp.asarray(drift_table(nha, chv // NV, nj))
        codes = jnp.pad(corner[0].T, ((0, 0), (0, 128 - CAP))).reshape(total, 1, 128)
        wts = weights[0].transpose(2, 1, 0).reshape(total, CAP * 16)
        wts = jnp.pad(wts, ((0, 0), (0, 128 - CAP * 16))).reshape(total, 1, 128)
        f32, i32 = jnp.float32, jnp.int32
        tiles = cy * (cx // 16) * 3
        dma = pltpu.SemaphoreType.DMA
        vmem = pl.BlockSpec(memory_space=pltpu.VMEM)
        any_ = pl.BlockSpec(memory_space=pl.ANY)
        final, samples = pl.pallas_call(
            functools.partial(kernel, (ngx, ngy, nha, cx, cy, nj)),
            out_shape=(jax.ShapeDtypeStruct((cx * cy, chv), f32),
                       jax.ShapeDtypeStruct((CAP, total), f32)),
            in_specs=[any_, vmem, vmem, vmem, vmem],
            out_specs=(any_, vmem),
            scratch_shapes=[
                pltpu.VMEM((STEPS + 1, cy + 2 * LO, cx + 2 * LO, 24, 128), f32),
                pltpu.VMEM((cy, cx, 8, 128), f32),
                pltpu.VMEM((cy, cx, 8, 128), f32),
                pltpu.VMEM((cx, 24, 128), f32),
                pltpu.VMEM((nj * cx * cy, 128), f32),
                pltpu.VMEM((STEPS, 2, CHUNKS, tiles // CHUNKS, 8, 128), f32),
                pltpu.VMEM((STEPS, 2, CHUNKS, tiles // CHUNKS, 8, 128), f32),
                pltpu.VMEM((total, 1, 128), i32),
                pltpu.VMEM((total, 1, 128), f32),
                pltpu.SMEM((total, 1, 128), i32),
                pltpu.SMEM((total, 1, 128), f32),
                pltpu.VMEM((total, CAP, 128), f32),
                pltpu.VMEM((total, CAP, 128), f32),
                pltpu.VMEM((total * CAP, 4, 8, 128), f32),
                dma((nj,)), dma((nj,)), dma((STEPS, 2 + 4 * CHUNKS)), dma((STEPS, 2 + 4 * CHUNKS)),
                dma((total,)), dma((total,)), dma((total,)), dma((total,)),
                dma((total,)), dma((total,)), dma((3,)),
            ],
            compiler_params=pltpu.CompilerParams(
                collective_id=0, has_side_effects=True, vmem_limit_bytes=56 * 1024 * 1024),
        )(initial_value.reshape(cx * cy, chv), codes, wts, table, corner[0])
        return (final.reshape(cx, cy, chv), samples[None])

    return jax.shard_map(
        local,
        mesh=mesh,
        in_specs=(P("gx", "gy", "ha"), P(("gx", "gy", "ha"), None, None),
                  P(("gx", "gy", "ha"), None, None, None)),
        out_specs=(P("gx", "gy", "ha"), P(("gx", "gy", "ha"), None, None)),
        check_vma=False,
    )
```

```python
import functools

import jax
import jax.numpy as jnp
import numpy as np
from jax import lax
from jax.experimental import pallas as pl
from jax.experimental.pallas import tpu as pltpu
from jax.sharding import PartitionSpec as P

NV = 64
STEPS = 4
CAP = 4
MESH = pl.DeviceIdType.MESH
EPS4 = 4e-6
DT = 0.15
LO, HI = 3, 2
CHUNKS = 4


def smooth(t):
    return (13.0 / 3.0) * (t * t) + EPS4


def square(v):
    return v * v


def terms(cells):
    n = len(cells)
    d = [cells[i + 1] - cells[i] for i in range(n - 1)]
    e = [d[i + 1] - d[i] for i in range(n - 2)]
    t = [e[i + 1] - e[i] for i in range(n - 3)]
    z = [t[i] - t[i + 1] for i in range(n - 4)]
    m = [smooth(v) for v in t]
    e3 = [3.0 * v for v in e]
    return d, e, z, m, e3


def products_at(i, e, m, e3):
    u1 = e3[i + 1] - e[i]
    u2 = e[i + 1] + e[i + 2]
    u3 = e3[i + 2] - e[i + 3]
    s1, s2, s3 = square(m[i] + u1 * u1), square(m[i + 1] + u2 * u2), square(m[i + 2] + u3 * u3)
    return s2 * s3, 6.0 * (s1 * s3), s1 * s2


def upwind_line(cells):
    d, e, z, m, e3 = terms(cells)
    out = []
    for i in range(len(cells) - 5):
        g1, g2, g3 = products_at(i, e, m, e3)
        g3 = 3.0 * g3
        num = (z[i] + z[i]) * g1 + z[i + 1] * g3
        lin = 6.0 * d[i + 2] + (e[i + 1] + (e[i + 2] + e[i + 2]))
        out.append(lin + num * pl.reciprocal(g1 + g2 + g3, approx=True))
    return out


def both_ways(cells):
    d, e, z, m, e3 = terms(cells)
    g1, g2, g3 = products_at(0, e, m, e3)
    c = 6.0 * d[2]
    h1, h3 = 3.0 * g1, 3.0 * g3
    forward = (c + (e[1] + (e[2] + e[2]))
               + ((z[0] + z[0]) * g1 + z[1] * h3) * pl.reciprocal(g1 + g2 + h3, approx=True))
    negated = ((e[2] + (e[1] + e[1])) - c
               + ((z[1] + z[1]) * g3 + z[0] * h1) * pl.reciprocal(h1 + g2 + g3, approx=True))
    return forward, negated


def kernel(sizes, v_hbm, code_ref, wt_ref, drift_ref, corner_ref, out_hbm, res_ref,
           grid, hx, hy, moved, turned, stage, send_h, recv_h, code_in, wt_in, code_s, wt_s, rows, res_in, wt_tile,
           in_sem, out_sem, halo_send, halo_recv, cs_sem, cr_sem, ws_sem, wr_sem, rs_sem, rr_sem, loc_sem):
    ngx, ngy, nha, cx, cy, nj = sizes
    total = ngx * ngy * nha
    gx, gy, ha = lax.axis_index("gx"), lax.axis_index("gy"), lax.axis_index("ha")
    me = (gx * ngy + gy) * nha + ha
    quarter = ha * 4 // nha
    east = (quarter == 0) | (quarter == 3)
    north = quarter < 2
    sx = jnp.where(east, 1, -1)
    sy = jnp.where(north, 1, -1)
    x0 = jnp.where(east, 0, cx - 1)
    y0 = jnp.where(north, 0, cy - 1)
    xb = jnp.where(east, 0, cx + 2 * LO - 1)
    yb = jnp.where(north, 0, cy + 2 * LO - 1)

    def near(forward, a, b, count):
        return pl.ds(jnp.where(forward, a, b), count)

    def up_dst(forward, c):
        return near(forward, 0, c + LO, LO)

    def up_src(forward, c):
        return near(forward, c, LO, LO)

    def down_dst(forward, c):
        return near(forward, c + LO, LO - HI, HI)

    def down_src(forward, c):
        return near(forward, LO, c + LO - HI, HI)


    def device_of(o):
        return (o // (ngy * nha), (o // nha) % ngy, o % nha)

    loads = [
        pltpu.make_async_copy(
            v_hbm.at[:, pl.ds(128 * j, 128)], stage.at[pl.ds(j * cx * cy, cx * cy)], in_sem.at[j])
        for j in range(nj)
    ]
    for c in loads:
        c.start()

    barrier = pltpu.get_barrier_semaphore()

    @pl.loop(1, total)
    def _(i):
        pl.semaphore_signal(barrier, inc=1, device_id=device_of((me + i) % total), device_id_type=MESH)

    tile0 = jnp.zeros((8, 128), jnp.float32)
    x_up = gx - sx
    x_down = gx + sx
    y_up = gy - sy
    y_down = gy + sy
    has_xu = (x_up >= 0) & (x_up < ngx)
    has_xd = (x_down >= 0) & (x_down < ngx)
    has_yu = (y_up >= 0) & (y_up < ngy)
    has_yd = (y_down >= 0) & (y_down < ngy)

    def zero_x(first, count):
        @pl.loop(0, STEPS)
        def _(n):
            @pl.loop(0, cy)
            def _(y):
                for x in range(count):
                    grid[n, y + LO, first + x, 8:16, :] = tile0

    def zero_y(first, count):
        @pl.loop(0, STEPS)
        def _(n):
            @pl.loop(0, cx)
            def _(x):
                for y in range(count):
                    grid[n, first + y, x + LO, 8:16, :] = tile0

    pl.when(jnp.logical_not(has_xu))(lambda: zero_x(jnp.where(east, 0, cx + LO), LO))
    pl.when(jnp.logical_not(has_xd))(lambda: zero_x(jnp.where(east, cx + LO, LO - HI), HI))
    pl.when(jnp.logical_not(has_yu))(lambda: zero_y(jnp.where(north, 0, cy + LO), LO))
    pl.when(jnp.logical_not(has_yd))(lambda: zero_y(jnp.where(north, cy + LO, LO - HI), HI))

    for c in loads:
        c.wait()

    @pl.loop(0, cy)
    def _(y):
        for x in range(cx):
            row = x * cy + y
            grid[0, y + LO, x + LO, 8:16, :] = stage[pl.ds(row, nj, stride=cx * cy), :]

    pl.semaphore_wait(barrier, total - 1)

    def request(o):
        return (
            pltpu.make_async_remote_copy(
                src_ref=code_ref.at[o], dst_ref=code_in.at[me], send_sem=cs_sem.at[o],
                recv_sem=cr_sem.at[me], device_id=device_of(o), device_id_type=MESH),
            pltpu.make_async_remote_copy(
                src_ref=wt_ref.at[o], dst_ref=wt_in.at[me], send_sem=ws_sem.at[o],
                recv_sem=wr_sem.at[me], device_id=device_of(o), device_id_type=MESH),
        )

    def request_from(o):
        return (
            pltpu.make_async_remote_copy(
                src_ref=code_ref.at[o], dst_ref=code_in.at[o], send_sem=cs_sem.at[o],
                recv_sem=cr_sem.at[o], device_id=device_of(o), device_id_type=MESH),
            pltpu.make_async_remote_copy(
                src_ref=wt_ref.at[o], dst_ref=wt_in.at[o], send_sem=ws_sem.at[o],
                recv_sem=wr_sem.at[o], device_id=device_of(o), device_id_type=MESH),
        )

    xs = pl.ds(LO, cx)
    depth = cy // CHUNKS

    def x_copies(n, c):
        g = grid.at[n]
        ys = pl.ds(LO + c * depth, depth)
        up = pltpu.make_async_remote_copy(
            src_ref=g.at[ys, up_src(east, cx), pl.ds(8, 8)], dst_ref=g.at[ys, up_dst(east, cx), pl.ds(8, 8)],
            send_sem=halo_send.at[n, 2 + c], recv_sem=halo_recv.at[n, 2 + c],
            device_id=(x_down, gy, ha), device_id_type=MESH)
        down = pltpu.make_async_remote_copy(
            src_ref=g.at[ys, down_src(east, cx), pl.ds(8, 8)], dst_ref=g.at[ys, down_dst(east, cx), pl.ds(8, 8)],
            send_sem=halo_send.at[n, 2 + CHUNKS + c], recv_sem=halo_recv.at[n, 2 + CHUNKS + c],
            device_id=(x_up, gy, ha), device_id_type=MESH)
        return up, down

    def y_copies(n):
        g = grid.at[n]
        up = pltpu.make_async_remote_copy(
            src_ref=g.at[up_src(north, cy), xs, pl.ds(8, 8)], dst_ref=g.at[up_dst(north, cy), xs, pl.ds(8, 8)],
            send_sem=halo_send.at[n, 0], recv_sem=halo_recv.at[n, 0],
            device_id=(gx, y_down, ha), device_id_type=MESH)
        down = pltpu.make_async_remote_copy(
            src_ref=g.at[down_src(north, cy), xs, pl.ds(8, 8)], dst_ref=g.at[down_dst(north, cy), xs, pl.ds(8, 8)],
            send_sem=halo_send.at[n, 1], recv_sem=halo_recv.at[n, 1],
            device_id=(gx, y_up, ha), device_id_type=MESH)
        return up, down

    def h_copies(n, c):
        return tuple(
            pltpu.make_async_remote_copy(
                src_ref=send_h.at[n, k, c], dst_ref=recv_h.at[n, k, c],
                send_sem=halo_send.at[n, 2 + (2 + k) * CHUNKS + c], recv_sem=halo_recv.at[n, 2 + (2 + k) * CHUNKS + c],
                device_id=(gx, gy, (ha + (1 if k == 0 else nha - 1)) % nha), device_id_type=MESH)
            for k in range(2))

    low_half = lax.broadcasted_iota(jnp.int32, (8, 128), 1) < NV

    def swap(v):
        return pltpu.roll(v, NV, 1)

    flat = grid.reshape(grid.shape[0] * grid.shape[1] * grid.shape[2] * 24, 128)

    moved_flat = moved.reshape(cx * 24, 128)
    turned_flat = turned.reshape(cx * 24, 128)

    def row_of(n, y, x, r):
        return ((n * (cy + 2 * LO) + y + LO) * (cx + 2 * LO) + x + LO) * 24 + r

    halves = cx // 16

    def pack(n, c, r):
        y = c * depth + r
        for q in range(2 * halves):
            send_h[n, 0, c, r * 2 * halves + q] = flat[pl.ds(row_of(n, y, 8 * q, 15), 8, stride=24), :]
            send_h[n, 1, c, r * 2 * halves + q] = flat[pl.ds(row_of(n, y, 8 * q, 8), 8, stride=24), :]
        for q in range(halves):
            at = (2 * depth + r) * halves + q
            a = flat[pl.ds(row_of(n, y, 16 * q, 14), 8, stride=24), :]
            b = flat[pl.ds(row_of(n, y, 16 * q + 8, 14), 8, stride=24), :]
            send_h[n, 0, c, at] = jnp.where(low_half, swap(a), b)
            a = flat[pl.ds(row_of(n, y, 16 * q, 9), 8, stride=24), :]
            b = flat[pl.ds(row_of(n, y, 16 * q + 8, 9), 8, stride=24), :]
            send_h[n, 1, c, at] = jnp.where(low_half, a, swap(b))

    def unpack(n, c, r):
        y = c * depth + r
        for q in range(2 * halves):
            flat[pl.ds(row_of(n, y, 8 * q, 7), 8, stride=24), :] = recv_h[n, 0, c, r * 2 * halves + q]
            flat[pl.ds(row_of(n, y, 8 * q, 16), 8, stride=24), :] = recv_h[n, 1, c, r * 2 * halves + q]
            turned_flat[pl.ds(8 * q * 24 + 7, 8, stride=24), :] = swap(recv_h[n, 0, c, r * 2 * halves + q])
            turned_flat[pl.ds(8 * q * 24 + 16, 8, stride=24), :] = swap(recv_h[n, 1, c, r * 2 * halves + q])
        for q in range(halves):
            at = (2 * depth + r) * halves + q
            v = recv_h[n, 0, c, at]
            here = [send_h[n, 1, c, r * 2 * halves + 2 * q + k] for k in range(2)]
            past = [recv_h[n, 0, c, r * 2 * halves + 2 * q + k] for k in range(2)]
            edge, _ = both_ways([
                v,
                jnp.where(low_half, past[0], swap(past[1])), jnp.where(low_half, swap(past[0]), past[1]),
                jnp.where(low_half, here[0], swap(here[1])), jnp.where(low_half, swap(here[0]), here[1]),
                send_h[n, 1, c, at],
            ])
            moved_flat[pl.ds(16 * q * 24 + 7, 8, stride=24), :] = edge
            moved_flat[pl.ds((16 * q + 8) * 24 + 7, 8, stride=24), :] = swap(edge)
            v = recv_h[n, 1, c, at]
            turned_flat[pl.ds(16 * q * 24 + 17, 8, stride=24), :] = swap(v)
            turned_flat[pl.ds((16 * q + 8) * 24 + 17, 8, stride=24), :] = v

    def send_chunk(n, c):
        for copy in h_copies(n, c):
            copy.start()

    def send_y(n, low):
        yu, yd = y_copies(n)
        up = jnp.logical_not(north) if low else north
        pl.when(up & has_yd)(lambda: yu.start())
        pl.when(jnp.logical_not(up) & has_yu)(lambda: yd.start())

    def send_x(n, c):
        xu, xd = x_copies(n, c)
        pl.when(has_xd)(lambda: xu.start())
        pl.when(has_xu)(lambda: xd.start())

    def chunk_at(i):
        return jnp.where(i < 2, i + 1, jnp.where(i == 2, 0, 3))

    send_y(0, True)
    send_y(0, False)

    @pl.loop(0, CHUNKS)
    def _(i):
        c = chunk_at(i)

        @pl.loop(0, depth)
        def _(r):
            pack(0, c, r)

        send_chunk(0, c)
        send_x(0, c)

    @pl.loop(1, total)
    def _(i):
        for c in request((me + i) % total):
            c.start()

    own = (pltpu.make_async_copy(code_ref.at[me], code_in.at[me], loc_sem.at[0]),
           pltpu.make_async_copy(wt_ref.at[me], wt_in.at[me], loc_sem.at[1]))
    for c in own:
        c.start()
    for c in own:
        c.wait()

    drift_x = drift_ref[ha, 0]
    drift_y = drift_ref[ha, 1]

    def y_part(n, first, count):
        @pl.loop(0, cx // 4)
        def _(q):
            for p in range(4):
                x = 4 * q + p
                line = upwind_line([grid[n, yb + sy * (first + i), x + LO, 8:16, :] for i in range(count + 5)])
                for k in range(count):
                    hy[y0 + sy * (first + k), x] = drift_y * line[k]

    def x_part(n, c):
        @pl.loop(0, depth)
        def _(r):
            y = c * depth + r
            line = upwind_line([grid[n, y + LO, xb + sx * i, 8:16, :] for i in range(cx + 5)])
            for k in range(cx):
                hx[y, x0 + sx * k] = drift_x * line[k]

    ramp = (lax.broadcasted_iota(jnp.int32, (8, 128), 0) * 128
            + lax.broadcasted_iota(jnp.int32, (8, 128), 1))
    hv = nj * 128

    def get_requests():
        @pl.loop(1, total)
        def _(i):
            for c in request_from((me + i) % total):
                c.wait()

        to_s = (pltpu.make_async_copy(code_in, code_s, loc_sem.at[0]),
                pltpu.make_async_copy(wt_in, wt_s, loc_sem.at[1]))
        for c in to_s:
            c.start()
        for c in to_s:
            c.wait()

    def weight_tiles(n):
        @pl.loop(0, total // STEPS)
        def _(q):
            o = n * (total // STEPS) + q
            for slot in range(CAP):
                at = ramp - lax.rem(jnp.maximum(code_s[o, 0, slot], 0), hv)
                hits = [at == off for off in (0, 1, NV, NV + 1)]
                for m in range(4):
                    w = jnp.zeros((8, 128), jnp.float32)
                    for k in range(4):
                        w = jnp.where(hits[k], wt_s[o, 0, slot * 16 + 4 * m + k], w)
                    wt_tile[o * CAP + slot, m] = w

    @pl.loop(0, STEPS)
    def _(n):
        @pl.loop(0, CHUNKS)
        def _(i):
            c = chunk_at(i)
            yu, yd = y_copies(n)
            pl.when((i == 2) & has_yu)(lambda: yu.wait_recv())
            pl.when((i == 2) & has_yd)(lambda: yd.wait_recv())
            y_part(n, depth * jnp.where(north, c, CHUNKS - 1 - c), depth)
            xu, xd = x_copies(n, c)
            pl.when(has_xu)(lambda: xu.wait_recv())
            pl.when(has_xd)(lambda: xd.wait_recv())
            x_part(n, c)
            for copy in h_copies(n, c):
                copy.wait_recv()

            @pl.loop(0, depth)
            def _(r):
                y = c * depth + r
                unpack(n, c, r)
                for x in range(cx):
                    g = [grid[n, y + LO, x + LO, pl.ds(k, 8), :] for k in range(7, 10)]
                    mid = swap(g[1])
                    turned[x, 8:16, :] = mid
                    s = [turned[x, 7:15, :], mid, turned[x, 9:17, :], turned[x, 10:18, :]]
                    odd = [jnp.where(low_half, s[k], s[k + 1]) for k in range(3)]
                    forward, negated = both_ways([g[0], odd[0], g[1], odd[1], g[2], odd[2]])
                    forward = swap(forward)
                    moved[x, 8:16, :] = forward
                    forward = jnp.where(low_half, moved[x, 7:15, :], forward)
                    term = jnp.minimum(forward, negated)
                    ham = hx[y, x] + hy[y, x] + (DT / 6.0) * term
                    grid[n + 1, y + LO, x + LO, 8:16, :] = g[1] - jnp.maximum(ham, 0.0)
                pl.when(n < STEPS - 1)(lambda: pack(n + 1, c, r))

            @pl.when(n == STEPS - 1)
            def _():
                @pl.loop(0, depth)
                def _(r):
                    y = c * depth + r
                    for x in range(cx):
                        stage[pl.ds(x * cy + y, nj, stride=cx * cy), :] = grid[STEPS, y + LO, x + LO, 8:16, :]

            @pl.when(n < STEPS - 1)
            def _():
                send_chunk(n + 1, c)
                send_x(n + 1, c)
                pl.when(i == 2)(lambda: send_y(n + 1, True))
                pl.when(i == 3)(lambda: send_y(n + 1, False))

            pl.when((n == 0) & (i == 2))(get_requests)
            pl.when(i == 2)(lambda: weight_tiles(n))

    stores = [
        pltpu.make_async_copy(
            stage.at[pl.ds(j * cx * cy, cx * cy)], out_hbm.at[:, pl.ds(128 * j, 128)], out_sem.at[j])
        for j in range(nj)
    ]
    for c in stores:
        c.start()

    def answer(o, slot_of):
        return pltpu.make_async_remote_copy(
            src_ref=rows.at[o], dst_ref=res_in.at[slot_of], send_sem=rs_sem.at[o],
            recv_sem=rr_sem.at[slot_of], device_id=device_of(o), device_id_type=MESH)

    @pl.loop(0, total)
    def _(i):
        o = (me + i + 1) % total
        for slot in range(CAP):
            c = jnp.maximum(code_s[o, 0, slot], 0)
            a = lax.div(c, cy * hv)
            b = lax.rem(lax.div(c, hv), cy)
            part = [wt_tile[o * CAP + slot, 2 * i1 + i2] * grid[STEPS, b + i2 + LO, a + i1 + LO, 8:16, :]
                    for i1 in range(2) for i2 in range(2)]
            acc = (part[0] + part[1]) + (part[2] + part[3])
            rows[o, slot:slot + 1, :] = jnp.sum(acc, axis=0, keepdims=True)
        pl.when(o != me)(lambda: answer(o, me).start())

    mine = pltpu.make_async_copy(rows.at[me], res_in.at[me], loc_sem.at[2])
    mine.start()
    mine.wait()

    @pl.loop(1, total)
    def _(i):
        o = (me + i) % total
        answer(o, o).wait()

    for slot in range(CAP):
        sums = jnp.sum(res_in[:, slot, :].T, axis=0, keepdims=True)
        res_ref[slot:slot + 1, :] = jnp.where(corner_ref[slot:slot + 1, :] >= 0, sums, 0.0)

    @pl.loop(0, STEPS)
    def _(n):
        yu, yd = y_copies(n)
        pl.when(has_yd)(lambda: yu.wait_send())
        pl.when(has_yu)(lambda: yd.wait_send())

        @pl.loop(0, CHUNKS)
        def _(c):
            xu, xd = x_copies(n, c)
            pl.when(has_xd)(lambda: xu.wait_send())
            pl.when(has_xu)(lambda: xd.wait_send())
            for copy in h_copies(n, c):
                copy.wait_send()

    for c in stores:
        c.wait()


def drift_table(nha, ch, nj):
    heads = nha * ch
    angle = np.arange(heads, dtype=np.int32).astype(np.float32) * np.float32(6.283185307179586 / heads)
    speed = np.float32(0.5) + np.arange(NV, dtype=np.float32) / np.float32(NV - 1)
    quarter = np.arange(heads) * 4 // heads
    sign_x = np.where((quarter == 0) | (quarter == 3), 1.0, -1.0).astype(np.float32)
    sign_y = np.where(quarter < 2, 1.0, -1.0).astype(np.float32)
    table = np.stack([(sign_x * np.cos(angle))[:, None] * speed, (sign_y * np.sin(angle))[:, None] * speed])
    table = table * np.float32(DT / 6.0)
    return table.reshape(2, nha, nj, 128).transpose(1, 0, 2, 3).astype(np.float32)


def solution(mesh):
    ngx, ngy, nha = (mesh.shape[k] for k in ("gx", "gy", "ha"))
    total = ngx * ngy * nha
    assert nha % 4 == 0 and total % STEPS == 0

    def local(initial_value, corner, weights):
        cx, cy, chv = initial_value.shape
        nj = chv // 128
        assert nj == 8 and cx % 16 == 0
        table = jnp.asarray(drift_table(nha, chv // NV, nj))
        codes = jnp.pad(corner[0].T, ((0, 0), (0, 128 - CAP))).reshape(total, 1, 128)
        wts = weights[0].transpose(2, 1, 0).reshape(total, CAP * 16)
        wts = jnp.pad(wts, ((0, 0), (0, 128 - CAP * 16))).reshape(total, 1, 128)
        f32, i32 = jnp.float32, jnp.int32
        tiles = cy * (cx // 16) * 3
        dma = pltpu.SemaphoreType.DMA
        vmem = pl.BlockSpec(memory_space=pltpu.VMEM)
        any_ = pl.BlockSpec(memory_space=pl.ANY)
        final, samples = pl.pallas_call(
            functools.partial(kernel, (ngx, ngy, nha, cx, cy, nj)),
            out_shape=(jax.ShapeDtypeStruct((cx * cy, chv), f32),
                       jax.ShapeDtypeStruct((CAP, total), f32)),
            in_specs=[any_, vmem, vmem, vmem, vmem],
            out_specs=(any_, vmem),
            scratch_shapes=[
                pltpu.VMEM((STEPS + 1, cy + 2 * LO, cx + 2 * LO, 24, 128), f32),
                pltpu.VMEM((cy, cx, 8, 128), f32),
                pltpu.VMEM((cy, cx, 8, 128), f32),
                pltpu.VMEM((cx, 24, 128), f32),
                pltpu.VMEM((cx, 24, 128), f32),
                pltpu.VMEM((nj * cx * cy, 128), f32),
                pltpu.VMEM((STEPS, 2, CHUNKS, tiles // CHUNKS, 8, 128), f32),
                pltpu.VMEM((STEPS, 2, CHUNKS, tiles // CHUNKS, 8, 128), f32),
                pltpu.VMEM((total, 1, 128), i32),
                pltpu.VMEM((total, 1, 128), f32),
                pltpu.SMEM((total, 1, 128), i32),
                pltpu.SMEM((total, 1, 128), f32),
                pltpu.VMEM((total, CAP, 128), f32),
                pltpu.VMEM((total, CAP, 128), f32),
                pltpu.VMEM((total * CAP, 4, 8, 128), f32),
                dma((nj,)), dma((nj,)), dma((STEPS, 2 + 4 * CHUNKS)), dma((STEPS, 2 + 4 * CHUNKS)),
                dma((total,)), dma((total,)), dma((total,)), dma((total,)),
                dma((total,)), dma((total,)), dma((3,)),
            ],
            compiler_params=pltpu.CompilerParams(
                collective_id=0, has_side_effects=True, vmem_limit_bytes=56 * 1024 * 1024),
        )(initial_value.reshape(cx * cy, chv), codes, wts, table, corner[0])
        return (final.reshape(cx, cy, chv), samples[None])

    return jax.shard_map(
        local,
        mesh=mesh,
        in_specs=(P("gx", "gy", "ha"), P(("gx", "gy", "ha"), None, None),
                  P(("gx", "gy", "ha"), None, None, None)),
        out_specs=(P("gx", "gy", "ha"), P(("gx", "gy", "ha"), None, None)),
        check_vma=False,
    )
```
